32 devices in a mesh: group: 8 (over y, x, core), dom: 4 (over z).
Axes of the slice: x: 2, y: 2, z: 4, core: 2. Of those that a mesh axis runs over, the one named last changes fastest.
Arguments:
- x_self: bfloat16 [32768, 256], P(('group', 'dom')), may hold values from -6 to 6
- x_src: bfloat16 [16384, 256], P(('group', 'dom')), may hold values from -6 to 6
- tiles: bfloat16 [768, 128, 128], P(('group', 'dom')), may hold values from -0.375 to 0.375
- slot_dest_row: int32 [768], P(('group', 'dom')), may hold values from 0 to 11
- block_col: int32 [768], P(('group', 'dom')), may hold values from 0 to 3
- block_count: int32 [32], P(('group', 'dom')), may hold values from 2 to 24, as said below
- mirror_count: int32 [32, 4], P(('group', 'dom')), may hold values from 0 to 128, as said below
- mirror_index: int32 [32, 4, 128], P(('group', 'dom')), may hold values from 0 to 1023
- cotangent: bfloat16 [32768, 256], P(('group', 'dom')), may hold values from -6 to 6
- w_self: bfloat16 [256, 256], replicated, may hold values from -0.375 to 0.375
- w_neigh: bfloat16 [256, 256], replicated, may hold values from -0.375 to 0.375
Outputs:
- out: bfloat16 [32768, 256], P(('group', 'dom'))
- dx_self: bfloat16 [32768, 256], P(('group', 'dom'))
- dx_src: bfloat16 [16384, 256], P(('group', 'dom'))
- grad_weight: float32 [512, 256], P('group')
The draws below stay inside these ranges and needn't reach their ends.
Inputs may be any that keep to these rules, and one draw needn't show every extreme that they name: `block_count`: at least 2 and at most 24 tile slots of a device are live; some device has all 24 live. `mirror_count`: at most 128 live rows from one peer; on some device every peer sends 128.
All inputs are finite; a program needn't handle non-finite values.
Results may differ from the reference program's by a relative error of at most 0.02.
Values may be sent and summed in bfloat16 or wider, within the bound.
A program may use at most 64 MiB of HBM per device.

```python
import math
import jax
import jax.numpy as jnp
from jax import lax

HIDDEN_WIDTH = 256
TILE_EDGE = 128
DEVICE_MASTERS = 1024
S_DEV = 512
MIRROR_SLOTS = 512
NB_DEV = 24
CAP = 128
MASTERS = 32768
SOURCES = 16384
TOTAL_TILE_SLOTS = 768
NDEV = 32
N_GROUP = 8
N_DOM = 4


def draw_block_count(key, part):
    device_count = N_GROUP * N_DOM
    first, second = jax.random.split(jax.random.fold_in(key, 11))
    counts = jax.random.randint(first, (device_count,), 2, NB_DEV + 1).astype(jnp.int32)
    where = jax.random.randint(second, (), 0, device_count)
    return counts.at[where].set(NB_DEV)


def draw_mirror_count(key, part):
    device_count = N_GROUP * N_DOM
    capacity = MIRROR_SLOTS // N_DOM
    first, second = jax.random.split(jax.random.fold_in(key, 23))
    counts = jax.random.randint(first, (device_count, N_DOM), 0, capacity + 1).astype(jnp.int32)
    where = jax.random.randint(second, (), 0, device_count)
    return counts.at[where].set(capacity)


def with_ends(result, own_key, least, top_value):
    shape = result.shape
    index_at = [jax.random.randint(jax.random.fold_in(own_key, axis), (), 0, shape[axis]) for axis in range(len(shape))]
    result = result.at[tuple(index_at)].set(least)
    longest = shape.index(max(shape))
    index_at[longest] = (index_at[longest] + 1) % shape[longest]
    return result.at[tuple(index_at)].set(top_value)


def spiked(result, rng, source, target, blocks, factor):
    owner, partner = [(jnp.arange(result.shape[axis_at]) // (result.shape[axis_at] // blocks)).reshape([-1 if axis == axis_at else 1 for axis in range(result.ndim)]) for axis_at in (source, target)]
    chosen = jax.random.permutation(rng, blocks)[partner]
    strong = (owner == chosen) | (owner == (partner + blocks // 2) % blocks)
    return jnp.where(strong, factor * result, result)


def block_levels(key, dims, shards, low, high):
    loudness, own = 1.0, jax.random.fold_in(key, 6)
    for axis_at, parts in shards:
        draws = jnp.exp(jax.random.uniform(jax.random.fold_in(own, axis_at), (parts,), jnp.float32, low / len(shards), high / len(shards)))
        loudness = loudness * jnp.repeat(draws, dims[axis_at] // parts).reshape([-1 if axis == axis_at else 1 for axis in range(len(dims))])
    return loudness


def scatter_about(own_key, extent, width, most, cuts=(), dtype=jnp.bfloat16):
    gain = block_levels(own_key, extent, cuts, -0.22, 0.18) if cuts else 1.0
    result = jax.random.normal(own_key, extent, jnp.float32) * width * gain
    return jnp.minimum(jnp.maximum(result, -most), most).astype(dtype)


def bell_draw_with(key, extent, spread, bound, cuts, heavy, kind=jnp.bfloat16):
    drawn = spread * jax.random.normal(key, extent, jnp.float32)
    if cuts:
        drawn = drawn * block_levels(key, extent, cuts, -0.22, 0.18)
    return jnp.clip(spiked(drawn, jax.random.fold_in(key, 3), *heavy), -bound, bound).astype(kind)


def setup_inputs(seed: int = 0) -> dict:
    streams_of = jax.random.split(jax.random.key(seed), 12)
    return {
        "x_self": bell_draw_with(streams_of[0], (MASTERS, HIDDEN_WIDTH), 1.0, 6.0, ((0, 32),), (0, 1, 32, 2.75)),
        "x_src": scatter_about(streams_of[1], (SOURCES, HIDDEN_WIDTH), 1.0, 6.0, ((0, 32),)),
        "tiles": scatter_about(streams_of[2], (TOTAL_TILE_SLOTS, TILE_EDGE, TILE_EDGE), (TILE_EDGE * 2) ** -0.5, 0.375, ((0, 32),)),
        "slot_dest_row": with_ends(jax.random.randint(streams_of[3], (TOTAL_TILE_SLOTS,), 0, (DEVICE_MASTERS + MIRROR_SLOTS) // TILE_EDGE), jax.random.fold_in(streams_of[3], 1), 0, ((DEVICE_MASTERS + MIRROR_SLOTS) // TILE_EDGE) - 1).astype(jnp.int32),
        "block_col": with_ends(jax.random.randint(streams_of[4], (TOTAL_TILE_SLOTS,), 0, S_DEV // TILE_EDGE), jax.random.fold_in(streams_of[4], 1), 0, (S_DEV // TILE_EDGE) - 1).astype(jnp.int32),
        "block_count": draw_block_count(jax.random.fold_in(streams_of[11], 71), 0),
        "mirror_count": draw_mirror_count(jax.random.fold_in(streams_of[11], 71), 0),
        "mirror_index": with_ends(jax.random.randint(streams_of[7], (NDEV, N_DOM, CAP), 0, DEVICE_MASTERS), jax.random.fold_in(streams_of[7], 1), 0, DEVICE_MASTERS - 1).astype(jnp.int32),
        "cotangent": scatter_about(streams_of[8], (MASTERS, HIDDEN_WIDTH), 1.0, 6.0, ((0, 32),)),
        "w_self": scatter_about(streams_of[9], (HIDDEN_WIDTH, HIDDEN_WIDTH), HIDDEN_WIDTH ** -0.5, 0.375),
        "w_neigh": scatter_about(streams_of[10], (HIDDEN_WIDTH, HIDDEN_WIDTH), HIDDEN_WIDTH ** -0.5, 0.375),
    }


def tile_partial(tiles_dev, rows_dev, cols_dev, count, source, row_tile_count):
    nblock = tiles_dev.shape[0]
    valid = (jnp.arange(nblock).astype(jnp.int32) < count).astype(jnp.float32)
    src_tiles = source.reshape(-1, TILE_EDGE, source.shape[1])[cols_dev]
    product = jnp.einsum('bij,bjd->bid', tiles_dev.astype(jnp.float32), src_tiles.astype(jnp.float32))
    onehot = (rows_dev[None, :] == jnp.arange(row_tile_count).astype(jnp.int32)[:, None]).astype(jnp.float32) * valid[None, :]
    return jnp.einsum('tb,bid->tid', onehot, product).reshape(row_tile_count * TILE_EDGE, -1)

def reference(x_self, x_src, tiles, slot_dest_row, block_col, block_count, mirror_count, mirror_index, cotangent, w_self, w_neigh):
    device_count = N_GROUP * N_DOM
    capacity = MIRROR_SLOTS // N_DOM
    row_tile_count = (DEVICE_MASTERS + MIRROR_SLOTS) // TILE_EDGE
    src_tiles = S_DEV // TILE_EDGE
    xs_all = x_self.reshape(device_count, DEVICE_MASTERS, HIDDEN_WIDTH)
    src_all = x_src.reshape(device_count, S_DEV, HIDDEN_WIDTH)
    tl_all = tiles.reshape(device_count, NB_DEV, TILE_EDGE, TILE_EDGE)
    br_all = slot_dest_row.reshape(device_count, NB_DEV)
    bc_all = block_col.reshape(device_count, NB_DEV)
    cot_all = cotangent.reshape(device_count, DEVICE_MASTERS, HIDDEN_WIDTH)

    def mirror_part(a):
        return tile_partial(a[0], a[1], a[2], a[3], a[4], row_tile_count)[DEVICE_MASTERS:]
    mirrors = lax.map(mirror_part, (tl_all, br_all, bc_all, block_count, src_all))
    received = mirrors.reshape(N_GROUP, N_DOM, N_DOM, capacity, HIDDEN_WIDTH).transpose(0, 2, 1, 3, 4).reshape(device_count, N_DOM, capacity, HIDDEN_WIDTH)
    masks = (jnp.arange(capacity).astype(jnp.int32)[None, None, :] < mirror_count[:, :, None]).astype(jnp.float32)

    def dense(carry, a):
        xs_d, tl_d, br_d, bc_d, cnt_d, src_d, rec_d, msk_d, idx_d, cot_d = a
        part = tile_partial(tl_d, br_d, bc_d, cnt_d, src_d, row_tile_count)[:DEVICE_MASTERS]
        rows = (rec_d * msk_d[..., None]).reshape(-1, HIDDEN_WIDTH)
        agg = (part + jnp.zeros((DEVICE_MASTERS, HIDDEN_WIDTH), jnp.float32).at[idx_d.reshape(-1)].add(rows)).astype(jnp.bfloat16)
        pre = jnp.dot(xs_d, w_self, preferred_element_type=jnp.float32) + jnp.dot(agg, w_neigh, preferred_element_type=jnp.float32)
        sig = jax.nn.sigmoid(pre)
        out_d = (pre * sig).astype(jnp.bfloat16)
        gpre = (cot_d.astype(jnp.float32) * sig * (1.0 + pre * (1.0 - sig))).astype(jnp.bfloat16)
        term = jnp.concatenate([jnp.dot(xs_d.T, gpre, preferred_element_type=jnp.float32), jnp.dot(agg.T, gpre, preferred_element_type=jnp.float32)], 0)
        dxs = jnp.dot(gpre, w_self.T, preferred_element_type=jnp.float32).astype(jnp.bfloat16)
        gagg = jnp.dot(gpre, w_neigh.T, preferred_element_type=jnp.float32).astype(jnp.bfloat16)
        back = gagg[idx_d] * msk_d[..., None].astype(jnp.bfloat16)
        return (carry + term, (out_d, dxs, gagg, back))
    start = jnp.zeros((2 * HIDDEN_WIDTH, HIDDEN_WIDTH), jnp.float32)
    total, (outs, dxs_all, gagg_all, backward_results) = lax.scan(dense, start, (xs_all, tl_all, br_all, bc_all, block_count, src_all, received, masks, mirror_index, cot_all))
    mirror_gradient_rows = backward_results.reshape(N_GROUP, N_DOM, N_DOM, capacity, HIDDEN_WIDTH).transpose(0, 2, 1, 3, 4).reshape(device_count, MIRROR_SLOTS, HIDDEN_WIDTH)

    def backward(a):
        tl_d, br_d, bc_d, cnt_d, gagg_d, gm_d = a
        valid = (jnp.arange(NB_DEV).astype(jnp.int32) < cnt_d).astype(jnp.float32)
        gdest = jnp.concatenate([gagg_d, gm_d], 0).reshape(row_tile_count, TILE_EDGE, HIDDEN_WIDTH)
        rowsel = gdest[br_d]
        contrib = jnp.einsum('bij,bid->bjd', tl_d.astype(jnp.float32), rowsel.astype(jnp.float32))
        onehot = (bc_d[None, :] == jnp.arange(src_tiles).astype(jnp.int32)[:, None]).astype(jnp.float32) * valid[None, :]
        return jnp.einsum('sb,bjd->sjd', onehot, contrib).reshape(S_DEV, HIDDEN_WIDTH).astype(jnp.bfloat16)
    dx_src = lax.map(backward, (tl_all, br_all, bc_all, block_count, gagg_all, mirror_gradient_rows))
    grad_weight = total * (1.0 / math.sqrt(DEVICE_MASTERS * device_count))
    return (outs.reshape(DEVICE_MASTERS * device_count, HIDDEN_WIDTH), dxs_all.reshape(DEVICE_MASTERS * device_count, HIDDEN_WIDTH), dx_src.reshape(S_DEV * device_count, HIDDEN_WIDTH), grad_weight)
```

```python
import functools

import jax
import jax.numpy as jnp
from jax import lax
from jax.experimental import pallas as pl
from jax.experimental.pallas import tpu as pltpu
from jax.sharding import PartitionSpec as P

TILE_EDGE = 128
VMEM_LIMIT = 24 * 2**20
MESH = pl.DeviceIdType.MESH
F32 = jnp.float32
BF16 = jnp.bfloat16


def dot(a, b):
    return jnp.dot(a, b, preferred_element_type=F32)


def dot_nt(a, b):
    return lax.dot_general(a, b, (((1,), (1,)), ((), ())), preferred_element_type=F32)


def adjacency_kernel(
    masters,
    dest_ref,
    col_ref,
    count_ref,
    tiles_hbm,
    x_src_hbm,
    adj_ref,
    mirror_ref,
    tiles_ref,
    x_src_ref,
    sums,
    load_sem,
):
    src_count = x_src_ref.shape[0] // TILE_EDGE
    row_tiles = adj_ref.shape[0] // TILE_EDGE
    load_tiles = pltpu.make_async_copy(tiles_hbm, tiles_ref, load_sem.at[0])
    load_tiles.start()
    load_src = pltpu.make_async_copy(x_src_hbm, x_src_ref, load_sem.at[1])
    load_src.start()
    sums[...] = jnp.zeros_like(sums)
    load_tiles.wait()
    load_src.wait()

    @pl.loop(0, count_ref[0])
    def _(b):
        at = dest_ref[b] * src_count + col_ref[b]
        sums[at] += tiles_ref[b].astype(F32)

    @pl.loop(0, row_tiles)
    def _(t):
        rows = pl.ds(pl.multiple_of(t * TILE_EDGE, TILE_EDGE), TILE_EDGE)
        for s in range(src_count):
            adj_ref[rows, s * TILE_EDGE : (s + 1) * TILE_EDGE] = sums[t * src_count + s].astype(BF16)

    mirror_ref[...] = dot(adj_ref[masters:, :], x_src_ref[...]).astype(BF16)


def layer_kernel(
    ndom,
    ngroup,
    capacity,
    factor,
    live_ref,
    index_hbm,
    adj_hbm,
    mirror_ref,
    x_self_hbm,
    x_src_hbm,
    cot_hbm,
    w_self_hbm,
    w_neigh_hbm,
    out_hbm,
    dx_self_hbm,
    dx_src_hbm,
    grad_ref,
    out,
    dx_self,
    dx_src,
    index3,
    index,
    adj,
    x_self,
    x_src,
    cot,
    w_self,
    w_neigh,
    adj_t,
    pick,
    pick_t,
    own,
    pre_self,
    agg,
    gpre,
    g_agg,
    dx_acc,
    received,
    back,
    mirror_grad,
    x_self_t,
    term,
    term_in,
    rows_out,
    rows_in,
    load_sem,
    store_sem,
    local_sem,
    send_a,
    recv_a,
    send_b,
    recv_b,
    send_g,
    recv_g,
    send_d,
    recv_d,
):
    me_d = lax.axis_index("dom")
    me_g = lax.axis_index("group")
    masters, width = x_self.shape
    slots = index.shape[1]
    nsrc = x_src.shape[0]
    grad_rows = term.shape[0] // ngroup
    chunk = 256

    barrier = pltpu.get_barrier_semaphore()
    for k in range(1, ndom):
        pl.semaphore_signal(
            barrier, inc=1, device_id={"dom": lax.rem(me_d + k, ndom)}, device_id_type=MESH
        )
    for k in range(1, ngroup):
        pl.semaphore_signal(
            barrier, inc=1, device_id={"group": lax.rem(me_g + k, ngroup)}, device_id_type=MESH
        )
    loads = [
        pltpu.make_async_copy(src, dst, load_sem.at[i])
        for i, (src, dst) in enumerate(
            [
                (index_hbm, index3),
                (x_self_hbm, x_self),
                (w_self_hbm, w_self),
                (x_src_hbm, x_src),
                (adj_hbm, adj),
                (w_neigh_hbm, w_neigh),
                (cot_hbm, cot),
            ]
        )
    ]
    for load in loads:
        load.start()
    pl.semaphore_wait(barrier, ndom + ngroup - 2)

    def part(ref, i, rows):
        return ref.at[pl.ds(pl.multiple_of(i * rows, 16), rows), :]

    def exchange(src, dst, rows, size, me, axis, send, recv):
        copies = []
        for k in range(1, size):
            to = lax.rem(me + k, size)
            copy = pltpu.make_async_remote_copy(
                src_ref=part(src, to, rows) if src is not rows_out else src,
                dst_ref=part(dst, me, rows),
                send_sem=send.at[k],
                recv_sem=recv.at[k],
                device_id={axis: to},
                device_id_type=MESH,
            )
            copy.start()
            copies.append(copy)
        return copies

    sent_a = exchange(mirror_ref, received, capacity, ndom, me_d, "dom", send_a, recv_a)
    keep_a = pltpu.make_async_copy(
        part(mirror_ref, me_d, capacity), part(received, me_d, capacity), local_sem.at[0]
    )
    keep_a.start()

    for load in loads:
        load.wait()
    lane = lax.broadcasted_iota(jnp.int32, (1, capacity), 1)
    for p in range(ndom):
        index[:, p * capacity : (p + 1) * capacity] = jnp.where(
            lane < live_ref[0, p], index3[0, p : p + 1, :], -1
        )
    index_row = index[...]

    @pl.loop(0, masters // chunk)
    def _(i):
        rows = pl.ds(pl.multiple_of(i * chunk, chunk), chunk)
        own[rows, :] = dot(adj[rows, :], x_src[...])
        pre_self[rows, :] = dot(x_self[rows, :], w_self[...])
        ids = lax.broadcasted_iota(jnp.int32, (chunk, slots), 0) + i * chunk
        pick[rows, :] = jnp.where(ids == index_row, 1.0, 0.0).astype(BF16)

    index_col = jnp.broadcast_to(index_row, (TILE_EDGE, slots)).T
    lanes = lax.broadcasted_iota(jnp.int32, (slots, TILE_EDGE), 1)
    for k in range(masters // TILE_EDGE):
        pick_t[:, k * TILE_EDGE : (k + 1) * TILE_EDGE] = jnp.where(
            lanes + k * TILE_EDGE == index_col, 1.0, 0.0
        ).astype(BF16)
    for k in range(masters // chunk):
        x_self_t[:, k * chunk : (k + 1) * chunk] = x_self[k * chunk : (k + 1) * chunk, :].T

    keep_a.wait()
    for copy in sent_a:
        copy.wait()

    for i in range(masters // chunk):
        rows = pl.ds(i * chunk, chunk)
        agg_rows = (own[rows, :] + dot(pick[rows, :], received[...])).astype(BF16)
        agg[rows, :] = agg_rows
        pre = pre_self[rows, :] + dot(agg_rows, w_neigh[...])
        s = jax.nn.sigmoid(pre)
        out[rows, :] = (pre * s).astype(BF16)
        g = (cot[rows, :].astype(F32) * s * (1.0 + pre * (1.0 - s))).astype(BF16)
        gpre[rows, :] = g
        g_agg[rows, :] = dot_nt(g, w_neigh[...]).astype(BF16)

    store_out = pltpu.make_async_copy(out, out_hbm, store_sem.at[0])
    store_out.start()

    term[:width, :] = dot(x_self_t[...], gpre[...]).astype(BF16)
    term[width:, :] = lax.dot_general(
        agg[...], gpre[...], (((0,), (0,)), ((), ())), preferred_element_type=F32
    ).astype(BF16)
    sent_g = exchange(term, term_in, grad_rows, ngroup, me_g, "group", send_g, recv_g)
    keep_g = pltpu.make_async_copy(
        part(term, me_g, grad_rows), part(term_in, me_g, grad_rows), local_sem.at[2]
    )
    keep_g.start()

    back[...] = dot(pick_t[...], g_agg[...]).astype(BF16)
    sent_b = exchange(back, mirror_grad, capacity, ndom, me_d, "dom", send_b, recv_b)
    keep_b = pltpu.make_async_copy(
        part(back, me_d, capacity), part(mirror_grad, me_d, capacity), local_sem.at[1]
    )
    keep_b.start()

    @pl.loop(0, masters // chunk)
    def _(i):
        rows = pl.ds(pl.multiple_of(i * chunk, chunk), chunk)
        dx_self[rows, :] = dot_nt(gpre[rows, :], w_self[...]).astype(BF16)

    store_dx_self = pltpu.make_async_copy(dx_self, dx_self_hbm, store_sem.at[1])
    store_dx_self.start()

    for k in range(masters // chunk):
        adj_t[:, k * chunk : (k + 1) * chunk] = adj[k * chunk : (k + 1) * chunk, :].T

    keep_g.wait()
    for copy in sent_g:
        copy.wait()
    total = term_in[:grad_rows, :].astype(F32)
    for j in range(1, ngroup):
        total = total + term_in[j * grad_rows : (j + 1) * grad_rows, :].astype(F32)
    rows_out[...] = total.astype(BF16)
    sent_d = exchange(rows_out, rows_in, grad_rows, ndom, me_d, "dom", send_d, recv_d)
    keep_d = pltpu.make_async_copy(rows_out, part(rows_in, me_d, grad_rows), local_sem.at[3])
    keep_d.start()

    for k in range(masters // chunk, adj.shape[0] // chunk):
        adj_t[:, k * chunk : (k + 1) * chunk] = adj[k * chunk : (k + 1) * chunk, :].T
    dx_acc[...] = dot(adj_t[:, :masters], g_agg[...])
    keep_b.wait()
    for copy in sent_b:
        copy.wait()
    dx_src[...] = (dx_acc[...] + dot(adj_t[:, masters:], mirror_grad[...])).astype(BF16)
    store_dx_src = pltpu.make_async_copy(dx_src, dx_src_hbm, store_sem.at[2])
    store_dx_src.start()

    keep_d.wait()
    for copy in sent_d:
        copy.wait()
    total = rows_in[:grad_rows, :].astype(F32)
    for j in range(1, ndom):
        total = total + rows_in[j * grad_rows : (j + 1) * grad_rows, :].astype(F32)
    grad_ref[...] = total * factor
    store_out.wait()
    store_dx_self.wait()
    store_dx_src.wait()


def results_kernel(*refs):
    sources, targets, stages = refs[:4], refs[4:8], refs[8:12]
    load_sem, store_sem = refs[12:]
    loads = [
        pltpu.make_async_copy(a, b, load_sem.at[i]) for i, (a, b) in enumerate(zip(sources, stages))
    ]
    stores = [
        pltpu.make_async_copy(a, b, store_sem.at[i]) for i, (a, b) in enumerate(zip(stages, targets))
    ]
    for load in loads:
        load.start()
    for load, store in zip(loads, stores):
        load.wait()
        store.start()
    for store in stores:
        store.wait()


def on_device(
    x_self,
    x_src,
    tiles,
    slot_dest_row,
    block_col,
    block_count,
    mirror_count,
    mirror_index,
    cotangent,
    w_self,
    w_neigh,
):
    masters, width = x_self.shape
    nsrc = x_src.shape[0]
    ndom = lax.axis_size("dom")
    ngroup = lax.axis_size("group")
    capacity = mirror_index.shape[2]
    slots = ndom * capacity
    dest = masters + slots
    grad_rows = 2 * width // ngroup
    smem = pl.BlockSpec(memory_space=pltpu.SMEM)
    vmem = pl.BlockSpec(memory_space=pltpu.VMEM)
    anywhere = pl.BlockSpec(memory_space=pl.ANY)
    hbm = pl.BlockSpec(memory_space=pltpu.HBM)

    adj, mirror = pl.pallas_call(
        functools.partial(adjacency_kernel, masters),
        out_shape=(
            jax.ShapeDtypeStruct((dest, nsrc), BF16),
            jax.ShapeDtypeStruct((slots, width), BF16),
        ),
        in_specs=[smem, smem, smem, hbm, hbm],
        out_specs=(vmem, vmem),
        scratch_shapes=[
            pltpu.VMEM(tiles.shape, BF16),
            pltpu.VMEM(x_src.shape, BF16),
            pltpu.VMEM((dest * nsrc // TILE_EDGE**2, TILE_EDGE, TILE_EDGE), F32),
            pltpu.SemaphoreType.DMA((2,)),
        ],
        compiler_params=pltpu.CompilerParams(vmem_limit_bytes=VMEM_LIMIT),
        name="adjacency",
    )(slot_dest_row, block_col, block_count, tiles, x_src)

    factor = float((masters * ngroup * ndom) ** -0.5)

    def rows16(n, m=width):
        return pltpu.VMEM((n, m), BF16)

    def dma(n):
        return pltpu.SemaphoreType.DMA((n,))

    result_shapes = (
        jax.ShapeDtypeStruct((masters, width), BF16),
        jax.ShapeDtypeStruct((masters, width), BF16),
        jax.ShapeDtypeStruct((nsrc, width), BF16),
        jax.ShapeDtypeStruct((grad_rows, width), F32),
    )
    results = pl.pallas_call(
        functools.partial(layer_kernel, ndom, ngroup, capacity, factor),
        out_shape=result_shapes,
        in_specs=[smem, hbm, anywhere, anywhere, hbm, hbm, hbm, hbm, hbm],
        out_specs=(hbm, hbm, hbm, vmem),
        scratch_shapes=[
            rows16(masters),
            rows16(masters),
            rows16(nsrc),
            pltpu.VMEM((1, ndom, capacity), jnp.int32),
            pltpu.VMEM((1, slots), jnp.int32),
            rows16(dest, nsrc),
            rows16(masters),
            rows16(nsrc),
            rows16(masters),
            rows16(width),
            rows16(width),
            rows16(nsrc, dest),
            rows16(masters, slots),
            rows16(slots, masters),
            pltpu.VMEM((masters, width), F32),
            pltpu.VMEM((masters, width), F32),
            rows16(masters),
            rows16(masters),
            rows16(masters),
            pltpu.VMEM((nsrc, width), F32),
            rows16(slots),
            rows16(slots),
            rows16(slots),
            rows16(width, masters),
            rows16(2 * width),
            rows16(2 * width),
            rows16(grad_rows),
            rows16(ndom * grad_rows),
            dma(7),
            dma(3),
            dma(4),
            dma(ndom),
            dma(ndom),
            dma(ndom),
            dma(ndom),
            dma(ngroup),
            dma(ngroup),
            dma(ndom),
            dma(ndom),
        ],
        compiler_params=pltpu.CompilerParams(
            collective_id=0, has_side_effects=True, vmem_limit_bytes=VMEM_LIMIT
        ),
        name="layer",
    )(mirror_count, mirror_index, adj, mirror, x_self, x_src, cotangent, w_self, w_neigh)
    return pl.pallas_call(
        results_kernel,
        out_shape=result_shapes,
        in_specs=[anywhere] * 4,
        out_specs=(hbm,) * 4,
        scratch_shapes=[pltpu.VMEM(shape.shape, shape.dtype) for shape in result_shapes]
        + [dma(4), dma(4)],
        compiler_params=pltpu.CompilerParams(vmem_limit_bytes=VMEM_LIMIT),
        name="results",
    )(*results)


def solution(mesh):
    return jax.shard_map(
        on_device,
        mesh=mesh,
        in_specs=(
            P(("group", "dom"), None),
            P(("group", "dom"), None),
            P(("group", "dom"), None, None),
            P(("group", "dom")),
            P(("group", "dom")),
            P(("group", "dom")),
            P(("group", "dom"), None),
            P(("group", "dom"), None, None),
            P(("group", "dom"), None),
            P(),
            P(),
        ),
        out_specs=(
            P(("group", "dom"), None),
            P(("group", "dom"), None),
            P(("group", "dom"), None),
            P("group", None),
        ),
        check_vma=False,
    )
```

```python
import functools

import jax
import jax.numpy as jnp
from jax import lax
from jax.experimental import pallas as pl
from jax.experimental.pallas import tpu as pltpu
from jax.sharding import PartitionSpec as P

TILE_EDGE = 128
VMEM_LIMIT = 48 * 2**20
MESH = pl.DeviceIdType.MESH
F32 = jnp.float32
BF16 = jnp.bfloat16


def dot(a, b):
    return jnp.dot(a, b, preferred_element_type=F32)


def dot_nt(a, b):
    return lax.dot_general(a, b, (((1,), (1,)), ((), ())), preferred_element_type=F32)


def dot_tn(a, b):
    return lax.dot_general(a, b, (((0,), (0,)), ((), ())), preferred_element_type=F32)


def layer_kernel(
    ndom,
    ngroup,
    capacity,
    factor,
    dest_hbm,
    col_hbm,
    count,
    live_hbm,
    index_hbm,
    tiles_hbm,
    x_src_hbm,
    x_self_hbm,
    cot_hbm,
    w_self_hbm,
    w_neigh_hbm,
    out,
    dx_self,
    dx_src,
    grad_ref,
    dest,
    col,
    live,
    index3,
    index,
    tiles,
    x_src,
    x_self,
    cot,
    w_self,
    w_neigh,
    chosen,
    forward,
    backward,
    pick,
    pick_t,
    mirror,
    own,
    pre_self,
    agg,
    gpre,
    g_rows,
    g_dest,
    mirror_grad,
    received,
    back,
    x_self_t,
    term,
    term_in,
    rows_out,
    rows_in,
    load_sem,
    local_sem,
    send_a,
    recv_a,
    send_b,
    recv_b,
    send_g,
    recv_g,
    send_d,
    recv_d,
):
    me_d = lax.axis_index("dom")
    me_g = lax.axis_index("group")
    masters, width = x_self.shape
    slots = index.shape[1]
    nblock = tiles.shape[0]
    nsrc = dx_src.shape[0]
    grad_rows = term.shape[0] // ngroup
    chunk = 256
    edge = TILE_EDGE
    master_tiles = masters // edge

    barrier = pltpu.get_barrier_semaphore()
    for k in range(1, ndom):
        pl.semaphore_signal(
            barrier, inc=1, device_id={"dom": lax.rem(me_d + k, ndom)}, device_id_type=MESH
        )
    for k in range(1, ngroup):
        pl.semaphore_signal(
            barrier, inc=1, device_id={"group": lax.rem(me_g + k, ngroup)}, device_id_type=MESH
        )
    pairs = [
        (dest_hbm, dest),
        (col_hbm, col),
        (x_src_hbm, x_src),
        (tiles_hbm, tiles),
        (live_hbm, live),
        (index_hbm, index3),
        (x_self_hbm, x_self),
        (w_self_hbm, w_self),
        (w_neigh_hbm, w_neigh),
        (cot_hbm, cot),
    ]
    loads = [pltpu.make_async_copy(a, b, load_sem.at[i]) for i, (a, b) in enumerate(pairs)]
    for load in loads:
        load.start()

    def part(ref, i, rows):
        return ref.at[pl.ds(pl.multiple_of(i * rows, 16), rows), :]

    def exchange(src, dst, rows, size, me, axis, send, recv):
        copies = []
        for k in range(1, size):
            to = lax.rem(me + k, size)
            copy = pltpu.make_async_remote_copy(
                src_ref=part(src, to, rows) if src is not rows_out else src,
                dst_ref=part(dst, me, rows),
                send_sem=send.at[k],
                recv_sem=recv.at[k],
                device_id={axis: to},
                device_id_type=MESH,
            )
            copy.start()
            copies.append(copy)
        return copies

    for load in loads[:4]:
        load.wait()
    row_of, col_of = [], []
    for b in range(nblock):
        alive = (b < count[0]).astype(jnp.int32)
        row_of.append(alive * (dest[b] + 1) - 1)
        col_of.append(alive * (col[b] + 1) - 1)
    for b in range(nblock):
        chosen[b * edge : (b + 1) * edge, :] = x_src[col[b]]

    def kept(tile, key, wanted):
        return tile * jnp.broadcast_to((key == wanted).astype(F32), tile.shape).astype(BF16)

    def spread(at, wanted):
        for b in range(nblock):
            forward[at * edge : (at + 1) * edge, b * edge : (b + 1) * edge] = kept(
                tiles[b], row_of[b], wanted
            )

    for m in range(slots // edge):
        spread(m, master_tiles + m)
    mirror[...] = dot(forward[:slots, :], chosen[...]).astype(BF16)

    pl.semaphore_wait(barrier, ndom + ngroup - 2)
    sent_a = exchange(mirror, received, capacity, ndom, me_d, "dom", send_a, recv_a)
    keep_a = pltpu.make_async_copy(
        part(mirror, me_d, capacity), part(received, me_d, capacity), local_sem.at[0]
    )
    keep_a.start()

    for load in loads[4:]:
        load.wait()
    lane = lax.broadcasted_iota(jnp.int32, (1, capacity), 1)
    for p in range(ndom):
        index[:, p * capacity : (p + 1) * capacity] = jnp.where(
            lane < live[0, p], index3[0, p : p + 1, :], -1
        )
    index_row = index[...]

    for m in range(master_tiles):
        spread(m, m)

    @pl.loop(0, masters // chunk)
    def _(i):
        rows = pl.ds(pl.multiple_of(i * chunk, chunk), chunk)
        own[rows, :] = dot(forward[rows, :], chosen[...])
        pre_self[rows, :] = dot(x_self[rows, :], w_self[...])
        ids = lax.broadcasted_iota(jnp.int32, (chunk, slots), 0) + i * chunk
        pick[rows, :] = jnp.where(ids == index_row, 1.0, 0.0).astype(BF16)

    index_col = jnp.broadcast_to(index_row, (edge, slots)).T
    lanes = lax.broadcasted_iota(jnp.int32, (slots, edge), 1)
    for k in range(masters // edge):
        pick_t[:, k * edge : (k + 1) * edge] = jnp.where(
            lanes + k * edge == index_col, 1.0, 0.0
        ).astype(BF16)
    for k in range(masters // chunk):
        x_self_t[:, k * chunk : (k + 1) * chunk] = x_self[k * chunk : (k + 1) * chunk, :].T

    keep_a.wait()
    for copy in sent_a:
        copy.wait()

    for i in range(masters // chunk):
        rows = pl.ds(i * chunk, chunk)
        agg_rows = (own[rows, :] + dot(pick[rows, :], received[...])).astype(BF16)
        agg[rows, :] = agg_rows
        pre = pre_self[rows, :] + dot(agg_rows, w_neigh[...])
        s = 0.5 * jnp.tanh(0.5 * pre) + 0.5
        value = pre * s
        out[rows, :] = value.astype(BF16)
        g = (cot[rows, :].astype(F32) * (s + value * (1.0 - s))).astype(BF16)
        gpre[rows, :] = g
        g_agg = dot_nt(g, w_neigh[...]).astype(BF16)
        g_rows[rows, :] = g_agg
        for k in range(chunk // edge):
            g_dest[i * chunk // edge + k] = g_agg[k * edge : (k + 1) * edge, :]

    term[:width, :] = dot(x_self_t[...], gpre[...]).astype(BF16)
    term[width:, :] = dot_tn(agg[...], gpre[...]).astype(BF16)
    sent_g = exchange(term, term_in, grad_rows, ngroup, me_g, "group", send_g, recv_g)
    keep_g = pltpu.make_async_copy(
        part(term, me_g, grad_rows), part(term_in, me_g, grad_rows), local_sem.at[2]
    )
    keep_g.start()

    back[...] = dot(pick_t[...], g_rows[...]).astype(BF16)
    sent_b = exchange(back, mirror_grad, capacity, ndom, me_d, "dom", send_b, recv_b)
    keep_b = pltpu.make_async_copy(
        part(back, me_d, capacity),
        part(mirror_grad, me_d, capacity),
        local_sem.at[1],
    )
    keep_b.start()

    @pl.loop(0, masters // chunk)
    def _(i):
        rows = pl.ds(pl.multiple_of(i * chunk, chunk), chunk)
        dx_self[rows, :] = dot_nt(gpre[rows, :], w_self[...]).astype(BF16)

    for b in range(nblock):
        turned = tiles[b].T
        for c in range(nsrc // edge):
            backward[c * edge : (c + 1) * edge, b * edge : (b + 1) * edge] = kept(
                turned, col_of[b], c
            )

    keep_g.wait()
    for copy in sent_g:
        copy.wait()
    total = term_in[:grad_rows, :].astype(F32)
    for j in range(1, ngroup):
        total = total + term_in[j * grad_rows : (j + 1) * grad_rows, :].astype(F32)
    rows_out[...] = total.astype(BF16)
    sent_d = exchange(rows_out, rows_in, grad_rows, ndom, me_d, "dom", send_d, recv_d)
    keep_d = pltpu.make_async_copy(rows_out, part(rows_in, me_d, grad_rows), local_sem.at[3])
    keep_d.start()

    keep_b.wait()
    for copy in sent_b:
        copy.wait()
    for k in range(slots // edge):
        g_dest[master_tiles + k] = mirror_grad[k * edge : (k + 1) * edge, :]
    for b in range(nblock):
        chosen[b * edge : (b + 1) * edge, :] = g_dest[dest[b]]
    dx_src[...] = dot(backward[...], chosen[...]).astype(BF16)

    keep_d.wait()
    for copy in sent_d:
        copy.wait()
    total = rows_in[:grad_rows, :].astype(F32)
    for j in range(1, ndom):
        total = total + rows_in[j * grad_rows : (j + 1) * grad_rows, :].astype(F32)
    grad_ref[...] = total * factor


def results_kernel(*refs):
    sources, targets, sem = refs[:4], refs[4:8], refs[8]
    stores = [pltpu.make_async_copy(a, b, sem.at[i]) for i, (a, b) in enumerate(zip(sources, targets))]
    for store in stores:
        store.start()
    for store in stores:
        store.wait()


def on_device(
    x_self,
    x_src,
    tiles,
    slot_dest_row,
    block_col,
    block_count,
    mirror_count,
    mirror_index,
    cotangent,
    w_self,
    w_neigh,
):
    masters, width = x_self.shape
    nsrc = x_src.shape[0]
    nblock = tiles.shape[0]
    ndom = lax.axis_size("dom")
    ngroup = lax.axis_size("group")
    capacity = mirror_index.shape[2]
    slots = ndom * capacity
    dest = masters + slots
    span = nblock * TILE_EDGE
    grad_rows = 2 * width // ngroup
    vmem = pl.BlockSpec(memory_space=pltpu.VMEM)
    anywhere = pl.BlockSpec(memory_space=pl.ANY)
    hbm = pl.BlockSpec(memory_space=pltpu.HBM)
    factor = float((masters * ngroup * ndom) ** -0.5)

    def rows16(n, m=width):
        return pltpu.VMEM((n, m), BF16)

    def rows32(n, m=width):
        return pltpu.VMEM((n, m), F32)

    def dma(n):
        return pltpu.SemaphoreType.DMA((n,))

    arguments = [
        pltpu.with_memory_space_constraint(a, pltpu.HBM)
        for a in (
            slot_dest_row,
            block_col,
            mirror_count,
            mirror_index,
            tiles,
            x_src.reshape(nsrc // TILE_EDGE, TILE_EDGE, width),
            x_self,
            cotangent,
            w_self,
            w_neigh,
        )
    ]
    arguments.insert(2, block_count)
    in_specs = [hbm] * len(arguments)
    in_specs[2] = pl.BlockSpec(memory_space=pltpu.SMEM)
    result_shapes = (
        jax.ShapeDtypeStruct((masters, width), BF16),
        jax.ShapeDtypeStruct((masters, width), BF16),
        jax.ShapeDtypeStruct((nsrc, width), BF16),
        jax.ShapeDtypeStruct((grad_rows, width), F32),
    )
    results = pl.pallas_call(
        functools.partial(layer_kernel, ndom, ngroup, capacity, factor),
        out_shape=result_shapes,
        in_specs=in_specs,
        out_specs=(vmem,) * 4,
        scratch_shapes=[
            pltpu.SMEM((nblock,), jnp.int32),
            pltpu.SMEM((nblock,), jnp.int32),
            pltpu.SMEM((1, ndom), jnp.int32),
            pltpu.VMEM((1, ndom, capacity), jnp.int32),
            pltpu.VMEM((1, slots), jnp.int32),
            pltpu.VMEM(tiles.shape, BF16),
            pltpu.VMEM((nsrc // TILE_EDGE, TILE_EDGE, width), BF16),
            rows16(masters),
            rows16(masters),
            rows16(width),
            rows16(width),
            rows16(span),
            rows16(max(masters, slots), span),
            rows16(nsrc, span),
            rows16(masters, slots),
            rows16(slots, masters),
            rows16(slots),
            rows32(masters),
            rows32(masters),
            rows16(masters),
            rows16(masters),
            rows16(masters),
            pltpu.VMEM((dest // TILE_EDGE, TILE_EDGE, width), BF16),
            rows16(slots),
            rows16(slots),
            rows16(slots),
            rows16(width, masters),
            rows16(2 * width),
            rows16(2 * width),
            rows16(grad_rows),
            rows16(ndom * grad_rows),
            dma(10),
            dma(4),
            dma(ndom),
            dma(ndom),
            dma(ndom),
            dma(ndom),
            dma(ngroup),
            dma(ngroup),
            dma(ndom),
            dma(ndom),
        ],
        compiler_params=pltpu.CompilerParams(
            collective_id=0, has_side_effects=True, vmem_limit_bytes=VMEM_LIMIT
        ),
        name="layer",
    )(*arguments)
    return pl.pallas_call(
        results_kernel,
        out_shape=result_shapes,
        in_specs=[anywhere] * 4,
        out_specs=(hbm,) * 4,
        scratch_shapes=[dma(4)],
        compiler_params=pltpu.CompilerParams(vmem_limit_bytes=VMEM_LIMIT),
        name="results",
    )(*results)


def solution(mesh):
    return jax.shard_map(
        on_device,
        mesh=mesh,
        in_specs=(
            P(("group", "dom"), None),
            P(("group", "dom"), None),
            P(("group", "dom"), None, None),
            P(("group", "dom")),
            P(("group", "dom")),
            P(("group", "dom")),
            P(("group", "dom"), None),
            P(("group", "dom"), None, None),
            P(("group", "dom"), None),
            P(),
            P(),
        ),
        out_specs=(
            P(("group", "dom"), None),
            P(("group", "dom"), None),
            P(("group", "dom"), None),
            P("group", None),
        ),
        check_vma=False,
    )
```

```python
import functools

import jax
import jax.numpy as jnp
from jax import lax
from jax.experimental import pallas as pl
from jax.experimental.pallas import tpu as pltpu
from jax.sharding import PartitionSpec as P

TILE_EDGE = 128
VMEM_LIMIT = 48 * 2**20
PARTS = 1
MESH = pl.DeviceIdType.MESH
F32 = jnp.float32
BF16 = jnp.bfloat16


def dot(a, b):
    return jnp.dot(a, b, preferred_element_type=F32)


def dot_nt(a, b):
    return lax.dot_general(a, b, (((1,), (1,)), ((), ())), preferred_element_type=F32)


def dot_tn(a, b):
    return lax.dot_general(a, b, (((0,), (0,)), ((), ())), preferred_element_type=F32)


def partner(me, k):
    bit = 1
    while bit <= k:
        if k & bit:
            me = me + bit - 2 * bit * ((me // bit) % 2)
        bit *= 2
    return me


def layer_kernel(
    ndom,
    ngroup,
    capacity,
    factor,
    dest_hbm,
    col_hbm,
    count,
    live_hbm,
    index_hbm,
    tiles_hbm,
    x_src_hbm,
    x_self_hbm,
    cot_hbm,
    w_self_hbm,
    w_neigh_hbm,
    out,
    dx_self,
    dx_src,
    grad_ref,
    dest,
    col,
    live,
    index3,
    index,
    tiles,
    x_src,
    x_self,
    cot,
    w_self,
    w_neigh,
    chosen,
    forward,
    backward,
    pick,
    pick_t,
    mirror,
    own,
    pre_self,
    agg,
    gpre,
    g_rows,
    g_dest,
    mirror_grad,
    received,
    back,
    x_self_t,
    term,
    term_in,
    rows_out,
    rows_in,
    load_sem,
    local_sem,
    send_a,
    recv_a,
    send_b,
    recv_b,
    send_g,
    recv_g,
    send_d,
    recv_d,
):
    me_d = lax.axis_index("dom")
    me_g = lax.axis_index("group")
    masters, width = x_self.shape
    slots = index.shape[1]
    nblock = tiles.shape[0]
    nsrc = dx_src.shape[0]
    parts = term_in.shape[0]
    grad_rows = term.shape[0] // ngroup
    piece = grad_rows // parts
    half = slots // 2
    chunk = 256
    edge = TILE_EDGE
    master_tiles = masters // edge

    barrier = pltpu.get_barrier_semaphore()
    for k in range(ndom - 1, 0, -1):
        pl.semaphore_signal(
            barrier, inc=1, device_id={"dom": partner(me_d, k)}, device_id_type=MESH
        )
    for k in range(ngroup - 1, 0, -1):
        pl.semaphore_signal(
            barrier, inc=1, device_id={"group": partner(me_g, k)}, device_id_type=MESH
        )
    pairs = [
        (dest_hbm, dest),
        (col_hbm, col),
        (x_src_hbm, x_src),
        (tiles_hbm, tiles),
        (live_hbm, live),
        (index_hbm, index3),
        (x_self_hbm, x_self),
        (w_self_hbm, w_self),
        (w_neigh_hbm, w_neigh),
        (cot_hbm, cot),
    ]
    loads = [pltpu.make_async_copy(a, b, load_sem.at[i]) for i, (a, b) in enumerate(pairs)]
    for load in loads:
        load.start()

    def part(ref, i, rows):
        return ref.at[pl.ds(pl.multiple_of(i * rows, 16), rows), :]

    def send(src, dst, axis, me, k, sent, got):
        copy = pltpu.make_async_remote_copy(
            src_ref=src,
            dst_ref=dst,
            send_sem=sent,
            recv_sem=got,
            device_id={axis: partner(me, k)},
            device_id_type=MESH,
        )
        copy.start()
        return copy

    for load in loads[:4]:
        load.wait()
    row_of, col_of = [], []
    for b in range(nblock):
        alive = (b < count[0]).astype(jnp.int32)
        row_of.append(alive * (dest[b] + 1) - 1)
        col_of.append(alive * (col[b] + 1) - 1)
    for b in range(nblock):
        chosen[b * edge : (b + 1) * edge, :] = x_src[col[b]]

    def kept(tile, key, wanted):
        return tile * jnp.broadcast_to((key == wanted).astype(F32), tile.shape).astype(BF16)

    def spread(at, wanted):
        for b in range(nblock):
            forward[at * edge : (at + 1) * edge, b * edge : (b + 1) * edge] = kept(
                tiles[b], row_of[b], wanted
            )

    for m in range(slots // edge):
        spread(m, master_tiles + m)
    mirror[...] = dot(forward[:slots, :], chosen[...]).astype(BF16)

    pl.semaphore_wait(barrier, ndom + ngroup - 2)
    sent_a = [None] * ndom
    for k in [*range(1, ndom // 2), *range(ndom - 1, ndom // 2 - 1, -1)]:
        sent_a[k] = send(
            part(mirror, partner(me_d, k), capacity),
            part(received, k, capacity),
            "dom",
            me_d,
            k,
            send_a.at[k],
            recv_a.at[k],
        )
    keep_a = pltpu.make_async_copy(
        part(mirror, me_d, capacity), part(received, 0, capacity), local_sem.at[0]
    )
    keep_a.start()

    for load in loads[4:]:
        load.wait()
    lane = lax.broadcasted_iota(jnp.int32, (1, capacity), 1)
    for k in range(ndom):
        p = partner(me_d, k)
        index[:, k * capacity : (k + 1) * capacity] = jnp.where(
            lane < live[0, p], index3[0, pl.ds(p, 1), :], -1
        )
    index_row = index[...]

    for m in range(master_tiles):
        spread(m, m)

    @pl.loop(0, masters // chunk)
    def _(i):
        rows = pl.ds(pl.multiple_of(i * chunk, chunk), chunk)
        own[rows, :] = dot(forward[rows, :], chosen[...])
        pre_self[rows, :] = dot(x_self[rows, :], w_self[...])
        ids = lax.broadcasted_iota(jnp.int32, (chunk, slots), 0) + i * chunk
        pick[rows, :] = jnp.where(ids == index_row, 1.0, 0.0).astype(BF16)

    index_col = jnp.broadcast_to(index_row, (edge, slots)).T
    lanes = lax.broadcasted_iota(jnp.int32, (slots, edge), 1)
    for k in range(masters // edge):
        pick_t[:, k * edge : (k + 1) * edge] = jnp.where(
            lanes + k * edge == index_col, 1.0, 0.0
        ).astype(BF16)
    for k in range(masters // chunk):
        x_self_t[:, k * chunk : (k + 1) * chunk] = x_self[k * chunk : (k + 1) * chunk, :].T

    keep_a.wait()
    for k in range(1, ndom // 2):
        sent_a[k].wait()

    @pl.loop(0, masters // chunk)
    def _(i):
        rows = pl.ds(pl.multiple_of(i * chunk, chunk), chunk)
        own[rows, :] += dot(pick[rows, :half], received[:half, :])

    for k in range(ndom // 2, ndom):
        sent_a[k].wait()

    for i in range(masters // chunk):
        rows = pl.ds(i * chunk, chunk)
        agg[rows, :] = (own[rows, :] + dot(pick[rows, half:], received[half:, :])).astype(BF16)
    for i in range(masters // chunk):
        rows = pl.ds(i * chunk, chunk)
        pre = pre_self[rows, :] + dot(agg[rows, :], w_neigh[...])
        s = 0.5 * jnp.tanh(0.5 * pre) + 0.5
        value = pre * s
        out[rows, :] = value.astype(BF16)
        gpre[rows, :] = (cot[rows, :].astype(F32) * (s + value * (1.0 - s))).astype(BF16)

    term[:width, :] = dot(x_self_t[...], gpre[...]).astype(BF16)
    term[width:, :] = dot_tn(agg[...], gpre[...]).astype(BF16)

    def piece_of(ref, i, j):
        return ref.at[pl.ds(pl.multiple_of(i * grad_rows + j * piece, 16), piece), :]

    sent_g = [
        [
            send(
                piece_of(term, partner(me_g, k), j),
                part(term_in.at[j], k, piece),
                "group",
                me_g,
                k,
                send_g.at[j, k],
                recv_g.at[j, k],
            )
            for k in range(ngroup - 1, 0, -1)
        ]
        for j in range(parts)
    ]

    for i in range(masters // chunk):
        rows = pl.ds(i * chunk, chunk)
        g_agg = dot_nt(gpre[rows, :], w_neigh[...]).astype(BF16)
        g_rows[rows, :] = g_agg
        for k in range(chunk // edge):
            g_dest[i * chunk // edge + k] = g_agg[k * edge : (k + 1) * edge, :]
    back[...] = dot(pick_t[...], g_rows[...]).astype(BF16)
    sent_b = [
        send(
            part(back, k, capacity),
            part(mirror_grad, me_d, capacity),
            "dom",
            me_d,
            k,
            send_b.at[k],
            recv_b.at[k],
        )
        for k in range(1, ndom)
    ]
    keep_b = pltpu.make_async_copy(
        part(back, 0, capacity), part(mirror_grad, me_d, capacity), local_sem.at[1]
    )
    keep_b.start()

    @pl.loop(0, masters // chunk)
    def _(i):
        rows = pl.ds(pl.multiple_of(i * chunk, chunk), chunk)
        dx_self[rows, :] = dot_nt(gpre[rows, :], w_self[...]).astype(BF16)

    for b in range(nblock):
        turned = tiles[b].T
        for c in range(nsrc // edge):
            backward[c * edge : (c + 1) * edge, b * edge : (b + 1) * edge] = kept(
                turned, col_of[b], c
            )

    sent_d = []
    for j in range(parts):
        for copy in sent_g[j]:
            copy.wait_recv()
        total = piece_of(term, me_g, j)[...].astype(F32)
        for k in range(1, ngroup):
            total = total + term_in[j, k * piece : (k + 1) * piece, :].astype(F32)
        rows_out[j] = total.astype(BF16)
        part(rows_in.at[j], me_d, piece)[...] = total.astype(BF16)
        sent_d += [
            send(
                rows_out.at[j],
                part(rows_in.at[j], me_d, piece),
                "dom",
                me_d,
                k,
                send_d.at[j, k],
                recv_d.at[j, k],
            )
            for k in range(1, ndom)
        ]
    for copies in sent_g:
        for copy in copies:
            copy.wait_send()

    keep_b.wait()
    for copy in sent_b:
        copy.wait()
    for k in range(slots // edge):
        g_dest[master_tiles + k] = mirror_grad[k * edge : (k + 1) * edge, :]
    for b in range(nblock):
        chosen[b * edge : (b + 1) * edge, :] = g_dest[dest[b]]
    dx_src[...] = dot(backward[...], chosen[...]).astype(BF16)

    for copy in sent_d:
        copy.wait()
    for j in range(parts):
        total = rows_in[j, :piece, :].astype(F32)
        for k in range(1, ndom):
            total = total + rows_in[j, k * piece : (k + 1) * piece, :].astype(F32)
        grad_ref[j * piece : (j + 1) * piece, :] = total * factor


def results_kernel(*refs):
    sources, targets, sem = refs[:4], refs[4:8], refs[8]
    stores = [pltpu.make_async_copy(a, b, sem.at[i]) for i, (a, b) in enumerate(zip(sources, targets))]
    for store in stores:
        store.start()
    for store in stores:
        store.wait()


def on_device(
    x_self,
    x_src,
    tiles,
    slot_dest_row,
    block_col,
    block_count,
    mirror_count,
    mirror_index,
    cotangent,
    w_self,
    w_neigh,
):
    masters, width = x_self.shape
    nsrc = x_src.shape[0]
    nblock = tiles.shape[0]
    ndom = lax.axis_size("dom")
    ngroup = lax.axis_size("group")
    capacity = mirror_index.shape[2]
    slots = ndom * capacity
    dest = masters + slots
    span = nblock * TILE_EDGE
    grad_rows = 2 * width // ngroup
    parts = max(1, min(PARTS, grad_rows // 16))
    piece = grad_rows // parts
    vmem = pl.BlockSpec(memory_space=pltpu.VMEM)
    anywhere = pl.BlockSpec(memory_space=pl.ANY)
    hbm = pl.BlockSpec(memory_space=pltpu.HBM)
    factor = float((masters * ngroup * ndom) ** -0.5)

    def rows16(n, m=width):
        return pltpu.VMEM((n, m), BF16)

    def rows32(n, m=width):
        return pltpu.VMEM((n, m), F32)

    def dma(*shape):
        return pltpu.SemaphoreType.DMA(shape)

    arguments = [
        pltpu.with_memory_space_constraint(a, pltpu.HBM)
        for a in (
            slot_dest_row,
            block_col,
            mirror_count,
            mirror_index,
            tiles,
            x_src.reshape(nsrc // TILE_EDGE, TILE_EDGE, width),
            x_self,
            cotangent,
            w_self,
            w_neigh,
        )
    ]
    arguments.insert(2, block_count)
    in_specs = [hbm] * len(arguments)
    in_specs[2] = pl.BlockSpec(memory_space=pltpu.SMEM)
    result_shapes = (
        jax.ShapeDtypeStruct((masters, width), BF16),
        jax.ShapeDtypeStruct((masters, width), BF16),
        jax.ShapeDtypeStruct((nsrc, width), BF16),
        jax.ShapeDtypeStruct((grad_rows, width), F32),
    )
    results = pl.pallas_call(
        functools.partial(layer_kernel, ndom, ngroup, capacity, factor),
        out_shape=result_shapes,
        in_specs=in_specs,
        out_specs=(vmem,) * 4,
        scratch_shapes=[
            pltpu.SMEM((nblock,), jnp.int32),
            pltpu.SMEM((nblock,), jnp.int32),
            pltpu.SMEM((1, ndom), jnp.int32),
            pltpu.VMEM((1, ndom, capacity), jnp.int32),
            pltpu.VMEM((1, slots), jnp.int32),
            pltpu.VMEM(tiles.shape, BF16),
            pltpu.VMEM((nsrc // TILE_EDGE, TILE_EDGE, width), BF16),
            rows16(masters),
            rows16(masters),
            rows16(width),
            rows16(width),
            rows16(span),
            rows16(max(masters, slots), span),
            rows16(nsrc, span),
            rows16(masters, slots),
            rows16(slots, masters),
            rows16(slots),
            rows32(masters),
            rows32(masters),
            rows16(masters),
            rows16(masters),
            rows16(masters),
            pltpu.VMEM((dest // TILE_EDGE, TILE_EDGE, width), BF16),
            rows16(slots),
            rows16(slots),
            rows16(slots),
            rows16(width, masters),
            rows16(2 * width),
            pltpu.VMEM((parts, ngroup * piece, width), BF16),
            pltpu.VMEM((parts, piece, width), BF16),
            pltpu.VMEM((parts, ndom * piece, width), BF16),
            dma(10),
            dma(2),
            dma(ndom),
            dma(ndom),
            dma(ndom),
            dma(ndom),
            dma(parts, ngroup),
            dma(parts, ngroup),
            dma(parts, ndom),
            dma(parts, ndom),
        ],
        compiler_params=pltpu.CompilerParams(
            collective_id=0, has_side_effects=True, vmem_limit_bytes=VMEM_LIMIT
        ),
        name="layer",
    )(*arguments)
    return pl.pallas_call(
        results_kernel,
        out_shape=result_shapes,
        in_specs=[anywhere] * 4,
        out_specs=(hbm,) * 4,
        scratch_shapes=[dma(4)],
        compiler_params=pltpu.CompilerParams(vmem_limit_bytes=VMEM_LIMIT),
        name="results",
    )(*results)


def solution(mesh):
    return jax.shard_map(
        on_device,
        mesh=mesh,
        in_specs=(
            P(("group", "dom"), None),
            P(("group", "dom"), None),
            P(("group", "dom"), None, None),
            P(("group", "dom")),
            P(("group", "dom")),
            P(("group", "dom")),
            P(("group", "dom"), None),
            P(("group", "dom"), None, None),
            P(("group", "dom"), None),
            P(),
            P(),
        ),
        out_specs=(
            P(("group", "dom"), None),
            P(("group", "dom"), None),
            P(("group", "dom"), None),
            P("group", None),
        ),
        check_vma=False,
    )
```

```python
import functools

import jax
import jax.numpy as jnp
from jax import lax
from jax.experimental import pallas as pl
from jax.experimental.pallas import tpu as pltpu
from jax.sharding import PartitionSpec as P

TILE_EDGE = 128
VMEM_LIMIT = 48 * 2**20
PARTS = 1
MESH = pl.DeviceIdType.MESH
F32 = jnp.float32
BF16 = jnp.bfloat16


def dot(a, b):
    return jnp.dot(a, b, preferred_element_type=F32)


def dot_nt(a, b):
    return lax.dot_general(a, b, (((1,), (1,)), ((), ())), preferred_element_type=F32)


def dot_tn(a, b):
    return lax.dot_general(a, b, (((0,), (0,)), ((), ())), preferred_element_type=F32)


def partner(me, k):
    bit = 1
    while bit <= k:
        if k & bit:
            me = me + bit - 2 * bit * ((me // bit) % 2)
        bit *= 2
    return me


def layer_kernel(
    ndom,
    ngroup,
    capacity,
    factor,
    dest_hbm,
    col_hbm,
    count,
    live_hbm,
    index_hbm,
    tiles_hbm,
    x_src_hbm,
    x_self_hbm,
    cot_hbm,
    w_self_hbm,
    w_neigh_hbm,
    out,
    dx_self,
    dx_src,
    grad_ref,
    dest,
    col,
    live,
    index3,
    index,
    tiles,
    x_src,
    x_self,
    cot,
    w_self,
    w_neigh,
    chosen,
    forward,
    backward,
    pick,
    pick_t,
    mirror,
    own,
    pre_self,
    agg,
    gpre,
    g_rows,
    g_dest,
    mirror_grad,
    received,
    back,
    x_self_t,
    term,
    term_in,
    rows_out,
    rows_in,
    load_sem,
    local_sem,
    send_a,
    recv_a,
    send_b,
    recv_b,
    send_g,
    recv_g,
    send_d,
    recv_d,
):
    me_d = lax.axis_index("dom")
    me_g = lax.axis_index("group")
    masters, width = x_self.shape
    slots = index.shape[1]
    nblock = tiles.shape[0]
    nsrc = dx_src.shape[0]
    parts = term_in.shape[0]
    grad_rows = term.shape[0] // ngroup
    piece = grad_rows // parts
    half = slots // 2
    chunk = 256
    edge = TILE_EDGE
    master_tiles = masters // edge

    pairs = [
        (dest_hbm, dest),
        (col_hbm, col),
        (x_src_hbm, x_src),
        (tiles_hbm, tiles),
        (live_hbm, live),
        (index_hbm, index3),
        (x_self_hbm, x_self),
        (w_self_hbm, w_self),
        (w_neigh_hbm, w_neigh),
        (cot_hbm, cot),
    ]
    loads = [pltpu.make_async_copy(a, b, load_sem.at[i]) for i, (a, b) in enumerate(pairs)]
    for load in loads[:4]:
        load.start()

    barrier = pltpu.get_barrier_semaphore()
    for k in range(ndom - 1, 0, -1):
        pl.semaphore_signal(
            barrier, inc=1, device_id={"dom": partner(me_d, k)}, device_id_type=MESH
        )
    for k in range(ngroup - 1, 0, -1):
        pl.semaphore_signal(
            barrier, inc=1, device_id={"group": partner(me_g, k)}, device_id_type=MESH
        )
    for load in loads[4:]:
        load.start()

    def part(ref, i, rows):
        return ref.at[pl.ds(pl.multiple_of(i * rows, 16), rows), :]

    def send(src, dst, axis, me, k, sent, got):
        copy = pltpu.make_async_remote_copy(
            src_ref=src,
            dst_ref=dst,
            send_sem=sent,
            recv_sem=got,
            device_id={axis: partner(me, k)},
            device_id_type=MESH,
        )
        copy.start()
        return copy

    for load in loads[:4]:
        load.wait()
    row_of, col_of = [], []
    for b in range(nblock):
        alive = (b < count[0]).astype(jnp.int32)
        row_of.append(alive * (dest[b] + 1) - 1)
        col_of.append(alive * (col[b] + 1) - 1)
    for b in range(nblock):
        chosen[b * edge : (b + 1) * edge, :] = x_src[col[b]]

    def kept(tile, key, wanted):
        return tile * jnp.broadcast_to((key == wanted).astype(F32), tile.shape).astype(BF16)

    def spread(at, wanted):
        for b in range(nblock):
            forward[at * edge : (at + 1) * edge, b * edge : (b + 1) * edge] = kept(
                tiles[b], row_of[b], wanted
            )

    for m in range(slots // edge):
        spread(m, master_tiles + m)
    mirror[...] = dot(forward[:slots, :], chosen[...]).astype(BF16)

    pl.semaphore_wait(barrier, ndom + ngroup - 2)
    sent_a = [None] * ndom
    for k in [*range(1, ndom // 2), *range(ndom - 1, ndom // 2 - 1, -1)]:
        sent_a[k] = send(
            part(mirror, partner(me_d, k), capacity),
            part(received, k, capacity),
            "dom",
            me_d,
            k,
            send_a.at[k],
            recv_a.at[k],
        )
    keep_a = pltpu.make_async_copy(
        part(mirror, me_d, capacity), part(received, 0, capacity), local_sem.at[0]
    )
    keep_a.start()

    for load in loads[4:]:
        load.wait()
    lane = lax.broadcasted_iota(jnp.int32, (1, capacity), 1)
    for k in range(ndom):
        p = partner(me_d, k)
        index[:, k * capacity : (k + 1) * capacity] = jnp.where(
            lane < live[0, p], index3[0, pl.ds(p, 1), :], -1
        )
    index_row = index[...]

    for m in range(master_tiles):
        spread(m, m)

    @pl.loop(0, masters // chunk)
    def _(i):
        rows = pl.ds(pl.multiple_of(i * chunk, chunk), chunk)
        own[rows, :] = dot(forward[rows, :], chosen[...])
        pre_self[rows, :] = dot(x_self[rows, :], w_self[...])
        ids = lax.broadcasted_iota(jnp.int32, (chunk, slots), 0) + i * chunk
        pick[rows, :] = jnp.where(ids == index_row, 1.0, 0.0).astype(BF16)

    index_col = jnp.broadcast_to(index_row, (edge, slots)).T
    lanes = lax.broadcasted_iota(jnp.int32, (slots, edge), 1)
    for k in range(masters // edge):
        pick_t[:, k * edge : (k + 1) * edge] = jnp.where(
            lanes + k * edge == index_col, 1.0, 0.0
        ).astype(BF16)
    for k in range(masters // chunk):
        x_self_t[:, k * chunk : (k + 1) * chunk] = x_self[k * chunk : (k + 1) * chunk, :].T

    keep_a.wait()
    for k in range(1, ndom // 2):
        sent_a[k].wait()

    @pl.loop(0, masters // chunk)
    def _(i):
        rows = pl.ds(pl.multiple_of(i * chunk, chunk), chunk)
        own[rows, :] += dot(pick[rows, :half], received[:half, :])

    for k in range(ndom // 2, ndom):
        sent_a[k].wait()

    for i in range(masters // chunk):
        rows = pl.ds(i * chunk, chunk)
        agg[rows, :] = (own[rows, :] + dot(pick[rows, half:], received[half:, :])).astype(BF16)
    for i in range(masters // chunk):
        rows = pl.ds(i * chunk, chunk)
        pre = pre_self[rows, :] + dot(agg[rows, :], w_neigh[...])
        s = 0.5 * jnp.tanh(0.5 * pre) + 0.5
        value = pre * s
        out[rows, :] = value.astype(BF16)
        gpre[rows, :] = (cot[rows, :].astype(F32) * (s + value * (1.0 - s))).astype(BF16)

    term[:width, :] = dot(x_self_t[...], gpre[...]).astype(BF16)
    term[width:, :] = dot_tn(agg[...], gpre[...]).astype(BF16)

    def piece_of(ref, i, j):
        return ref.at[pl.ds(pl.multiple_of(i * grad_rows + j * piece, 16), piece), :]

    sent_g = [
        [
            send(
                piece_of(term, partner(me_g, k), j),
                part(term_in.at[j], k, piece),
                "group",
                me_g,
                k,
                send_g.at[j, k],
                recv_g.at[j, k],
            )
            for k in range(ngroup - 1, 0, -1)
        ]
        for j in range(parts)
    ]

    for i in range(masters // chunk):
        rows = pl.ds(i * chunk, chunk)
        g_agg = dot_nt(gpre[rows, :], w_neigh[...]).astype(BF16)
        g_rows[rows, :] = g_agg
        for k in range(chunk // edge):
            g_dest[i * chunk // edge + k] = g_agg[k * edge : (k + 1) * edge, :]
    back[...] = dot(pick_t[...], g_rows[...]).astype(BF16)
    sent_b = [
        send(
            part(back, k, capacity),
            part(mirror_grad, me_d, capacity),
            "dom",
            me_d,
            k,
            send_b.at[k],
            recv_b.at[k],
        )
        for k in [ndom // 2, *[k for i in range(1, ndom // 2) for k in (i, ndom // 2 + i)]]
    ]
    keep_b = pltpu.make_async_copy(
        part(back, 0, capacity), part(mirror_grad, me_d, capacity), local_sem.at[1]
    )
    keep_b.start()

    @pl.loop(0, masters // chunk)
    def _(i):
        rows = pl.ds(pl.multiple_of(i * chunk, chunk), chunk)
        dx_self[rows, :] = dot_nt(gpre[rows, :], w_self[...]).astype(BF16)

    for b in range(nblock):
        turned = tiles[b].T
        for c in range(nsrc // edge):
            backward[c * edge : (c + 1) * edge, b * edge : (b + 1) * edge] = kept(
                turned, col_of[b], c
            )

    sent_d = []
    for j in range(parts):
        for copy in sent_g[j]:
            copy.wait_recv()
        total = piece_of(term, me_g, j)[...].astype(F32)
        for k in range(1, ngroup):
            total = total + term_in[j, k * piece : (k + 1) * piece, :].astype(F32)
        rows_out[j] = total.astype(BF16)
        part(rows_in.at[j], me_d, piece)[...] = total.astype(BF16)
        sent_d += [
            send(
                rows_out.at[j],
                part(rows_in.at[j], me_d, piece),
                "dom",
                me_d,
                k,
                send_d.at[j, k],
                recv_d.at[j, k],
            )
            for k in range(1, ndom)
        ]
    for copies in sent_g:
        for copy in copies:
            copy.wait_send()

    keep_b.wait()
    for copy in sent_b:
        copy.wait()
    for k in range(slots // edge):
        g_dest[master_tiles + k] = mirror_grad[k * edge : (k + 1) * edge, :]
    for b in range(nblock):
        chosen[b * edge : (b + 1) * edge, :] = g_dest[dest[b]]
    dx_src[...] = dot(backward[...], chosen[...]).astype(BF16)

    for copy in sent_d:
        copy.wait()
    for j in range(parts):
        total = rows_in[j, :piece, :].astype(F32)
        for k in range(1, ndom):
            total = total + rows_in[j, k * piece : (k + 1) * piece, :].astype(F32)
        grad_ref[j * piece : (j + 1) * piece, :] = total * factor


def results_kernel(*refs):
    sources, targets, sem = refs[:4], refs[4:8], refs[8]
    stores = [pltpu.make_async_copy(a, b, sem.at[i]) for i, (a, b) in enumerate(zip(sources, targets))]
    for store in stores:
        store.start()
    for store in stores:
        store.wait()


def on_device(
    x_self,
    x_src,
    tiles,
    slot_dest_row,
    block_col,
    block_count,
    mirror_count,
    mirror_index,
    cotangent,
    w_self,
    w_neigh,
):
    masters, width = x_self.shape
    nsrc = x_src.shape[0]
    nblock = tiles.shape[0]
    ndom = lax.axis_size("dom")
    ngroup = lax.axis_size("group")
    capacity = mirror_index.shape[2]
    slots = ndom * capacity
    dest = masters + slots
    span = nblock * TILE_EDGE
    grad_rows = 2 * width // ngroup
    parts = max(1, min(PARTS, grad_rows // 16))
    piece = grad_rows // parts
    vmem = pl.BlockSpec(memory_space=pltpu.VMEM)
    anywhere = pl.BlockSpec(memory_space=pl.ANY)
    hbm = pl.BlockSpec(memory_space=pltpu.HBM)
    factor = float((masters * ngroup * ndom) ** -0.5)

    def rows16(n, m=width):
        return pltpu.VMEM((n, m), BF16)

    def rows32(n, m=width):
        return pltpu.VMEM((n, m), F32)

    def dma(*shape):
        return pltpu.SemaphoreType.DMA(shape)

    arguments = [
        pltpu.with_memory_space_constraint(a, pltpu.HBM)
        for a in (
            slot_dest_row,
            block_col,
            mirror_count,
            mirror_index,
            tiles,
            x_src.reshape(nsrc // TILE_EDGE, TILE_EDGE, width),
            x_self,
            cotangent,
            w_self,
            w_neigh,
        )
    ]
    arguments.insert(2, block_count)
    in_specs = [hbm] * len(arguments)
    in_specs[2] = pl.BlockSpec(memory_space=pltpu.SMEM)
    result_shapes = (
        jax.ShapeDtypeStruct((masters, width), BF16),
        jax.ShapeDtypeStruct((masters, width), BF16),
        jax.ShapeDtypeStruct((nsrc, width), BF16),
        jax.ShapeDtypeStruct((grad_rows, width), F32),
    )
    results = pl.pallas_call(
        functools.partial(layer_kernel, ndom, ngroup, capacity, factor),
        out_shape=result_shapes,
        in_specs=in_specs,
        out_specs=(vmem,) * 4,
        scratch_shapes=[
            pltpu.SMEM((nblock,), jnp.int32),
            pltpu.SMEM((nblock,), jnp.int32),
            pltpu.SMEM((1, ndom), jnp.int32),
            pltpu.VMEM((1, ndom, capacity), jnp.int32),
            pltpu.VMEM((1, slots), jnp.int32),
            pltpu.VMEM(tiles.shape, BF16),
            pltpu.VMEM((nsrc // TILE_EDGE, TILE_EDGE, width), BF16),
            rows16(masters),
            rows16(masters),
            rows16(width),
            rows16(width),
            rows16(span),
            rows16(max(masters, slots), span),
            rows16(nsrc, span),
            rows16(masters, slots),
            rows16(slots, masters),
            rows16(slots),
            rows32(masters),
            rows32(masters),
            rows16(masters),
            rows16(masters),
            rows16(masters),
            pltpu.VMEM((dest // TILE_EDGE, TILE_EDGE, width), BF16),
            rows16(slots),
            rows16(slots),
            rows16(slots),
            rows16(width, masters),
            rows16(2 * width),
            pltpu.VMEM((parts, ngroup * piece, width), BF16),
            pltpu.VMEM((parts, piece, width), BF16),
            pltpu.VMEM((parts, ndom * piece, width), BF16),
            dma(10),
            dma(2),
            dma(ndom),
            dma(ndom),
            dma(ndom),
            dma(ndom),
            dma(parts, ngroup),
            dma(parts, ngroup),
            dma(parts, ndom),
            dma(parts, ndom),
        ],
        compiler_params=pltpu.CompilerParams(
            collective_id=0, has_side_effects=True, vmem_limit_bytes=VMEM_LIMIT
        ),
        name="layer",
    )(*arguments)
    return pl.pallas_call(
        results_kernel,
        out_shape=result_shapes,
        in_specs=[anywhere] * 4,
        out_specs=(hbm,) * 4,
        scratch_shapes=[dma(4)],
        compiler_params=pltpu.CompilerParams(vmem_limit_bytes=VMEM_LIMIT),
        name="results",
    )(*results)


def solution(mesh):
    return jax.shard_map(
        on_device,
        mesh=mesh,
        in_specs=(
            P(("group", "dom"), None),
            P(("group", "dom"), None),
            P(("group", "dom"), None, None),
            P(("group", "dom")),
            P(("group", "dom")),
            P(("group", "dom")),
            P(("group", "dom"), None),
            P(("group", "dom"), None, None),
            P(("group", "dom"), None),
            P(),
            P(),
        ),
        out_specs=(
            P(("group", "dom"), None),
            P(("group", "dom"), None),
            P(("group", "dom"), None),
            P("group", None),
        ),
        check_vma=False,
    )
```

```python
import functools

import jax
import jax.numpy as jnp
from jax import lax
from jax.experimental import pallas as pl
from jax.experimental.pallas import tpu as pltpu
from jax.sharding import PartitionSpec as P

TILE_EDGE = 128
VMEM_LIMIT = 48 * 2**20
PARTS = 1
MESH = pl.DeviceIdType.MESH
F32 = jnp.float32
BF16 = jnp.bfloat16


def dot(a, b):
    return jnp.dot(a, b, preferred_element_type=F32)


def dot_nt(a, b):
    return lax.dot_general(a, b, (((1,), (1,)), ((), ())), preferred_element_type=F32)


def dot_tn(a, b):
    return lax.dot_general(a, b, (((0,), (0,)), ((), ())), preferred_element_type=F32)


def partner(me, k):
    bit = 1
    while bit <= k:
        if k & bit:
            me = me + bit - 2 * bit * ((me // bit) % 2)
        bit *= 2
    return me


def layer_kernel(
    ndom,
    ngroup,
    capacity,
    factor,
    dest_hbm,
    col_hbm,
    count,
    live_hbm,
    index_hbm,
    tiles_hbm,
    x_src_hbm,
    x_self_hbm,
    cot_hbm,
    w_self_hbm,
    w_neigh_hbm,
    out,
    dx_self,
    dx_src,
    grad_ref,
    dest,
    col,
    live,
    index3,
    index,
    tiles,
    x_src,
    x_self,
    cot,
    w_self,
    w_neigh,
    chosen,
    forward,
    backward,
    pick,
    pick_t,
    mirror,
    own,
    pre_self,
    agg,
    gpre,
    g_rows,
    g_dest,
    mirror_grad,
    received,
    back,
    x_self_t,
    term,
    term_in,
    rows_out,
    rows_in,
    load_sem,
    local_sem,
    send_a,
    recv_a,
    send_b,
    recv_b,
    send_g,
    recv_g,
    send_d,
    recv_d,
):
    me_d = lax.axis_index("dom")
    me_g = lax.axis_index("group")
    masters, width = x_self.shape
    slots = index.shape[1]
    nblock = tiles.shape[0]
    nsrc = dx_src.shape[0]
    parts = term_in.shape[0]
    grad_rows = term.shape[0] // ngroup
    piece = grad_rows // parts
    half = slots // 2
    chunk = 256
    edge = TILE_EDGE
    master_tiles = masters // edge

    pairs = [
        (dest_hbm, dest),
        (col_hbm, col),
        (x_src_hbm, x_src),
        (tiles_hbm, tiles),
        (live_hbm, live),
        (index_hbm, index3),
        (x_self_hbm, x_self),
        (w_self_hbm, w_self),
        (w_neigh_hbm, w_neigh),
        (cot_hbm, cot),
    ]
    loads = [pltpu.make_async_copy(a, b, load_sem.at[i]) for i, (a, b) in enumerate(pairs)]
    for load in loads[:4]:
        load.start()

    barrier = pltpu.get_barrier_semaphore()
    for k in range(ndom - 1, 0, -1):
        pl.semaphore_signal(
            barrier, inc=1, device_id={"dom": partner(me_d, k)}, device_id_type=MESH
        )
    for k in range(ngroup - 1, 0, -1):
        pl.semaphore_signal(
            barrier, inc=1, device_id={"group": partner(me_g, k)}, device_id_type=MESH
        )
    for load in loads[4:]:
        load.start()

    def part(ref, i, rows):
        return ref.at[pl.ds(pl.multiple_of(i * rows, 16), rows), :]

    def send(src, dst, axis, me, k, sent, got):
        copy = pltpu.make_async_remote_copy(
            src_ref=src,
            dst_ref=dst,
            send_sem=sent,
            recv_sem=got,
            device_id={axis: partner(me, k)},
            device_id_type=MESH,
        )
        copy.start()
        return copy

    for load in loads[:4]:
        load.wait()
    row_of, col_of = [], []
    for b in range(nblock):
        alive = (b < count[0]).astype(jnp.int32)
        row_of.append(alive * (dest[b] + 1) - 1)
        col_of.append(alive * (col[b] + 1) - 1)
    for b in range(nblock):
        chosen[b * edge : (b + 1) * edge, :] = x_src[col[b]]

    def kept(tile, key, wanted):
        return tile * jnp.broadcast_to((key == wanted).astype(F32), tile.shape).astype(BF16)

    def spread(at, wanted):
        for b in range(nblock):
            forward[at * edge : (at + 1) * edge, b * edge : (b + 1) * edge] = kept(
                tiles[b], row_of[b], wanted
            )

    for m in range(slots // edge):
        spread(m, master_tiles + m)
    mirror[...] = dot(forward[:slots, :], chosen[...]).astype(BF16)

    pl.semaphore_wait(barrier, ndom + ngroup - 2)
    sent_a = [None] * ndom
    for k in [*range(1, ndom // 2), *range(ndom - 1, ndom // 2 - 1, -1)]:
        sent_a[k] = send(
            part(mirror, partner(me_d, k), capacity),
            part(received, k, capacity),
            "dom",
            me_d,
            k,
            send_a.at[k],
            recv_a.at[k],
        )
    keep_a = pltpu.make_async_copy(
        part(mirror, me_d, capacity), part(received, 0, capacity), local_sem.at[0]
    )
    keep_a.start()

    for load in loads[4:]:
        load.wait()
    lane = lax.broadcasted_iota(jnp.int32, (1, capacity), 1)
    for k in range(ndom):
        p = partner(me_d, k)
        index[:, k * capacity : (k + 1) * capacity] = jnp.where(
            lane < live[0, p], index3[0, pl.ds(p, 1), :], -1
        )
    index_row = index[...]

    for m in range(master_tiles):
        spread(m, m)

    @pl.loop(0, masters // chunk)
    def _(i):
        rows = pl.ds(pl.multiple_of(i * chunk, chunk), chunk)
        own[rows, :] = dot(forward[rows, :], chosen[...])
        pre_self[rows, :] = dot(x_self[rows, :], w_self[...])
        ids = lax.broadcasted_iota(jnp.int32, (chunk, slots), 0) + i * chunk
        pick[rows, :] = jnp.where(ids == index_row, 1.0, 0.0).astype(BF16)

    index_col = jnp.broadcast_to(index_row, (edge, slots)).T
    lanes = lax.broadcasted_iota(jnp.int32, (slots, edge), 1)
    for k in range(masters // edge):
        pick_t[:, k * edge : (k + 1) * edge] = jnp.where(
            lanes + k * edge == index_col, 1.0, 0.0
        ).astype(BF16)
    for k in range(masters // chunk):
        x_self_t[:, k * chunk : (k + 1) * chunk] = x_self[k * chunk : (k + 1) * chunk, :].T

    keep_a.wait()
    for k in range(1, ndom // 2):
        sent_a[k].wait()

    @pl.loop(0, masters // chunk)
    def _(i):
        rows = pl.ds(pl.multiple_of(i * chunk, chunk), chunk)
        own[rows, :] += dot(pick[rows, :half], received[:half, :])

    for k in range(ndom // 2, ndom):
        sent_a[k].wait()

    for i in range(masters // chunk):
        rows = pl.ds(i * chunk, chunk)
        agg[rows, :] = (own[rows, :] + dot(pick[rows, half:], received[half:, :])).astype(BF16)
    for i in range(masters // chunk):
        rows = pl.ds(i * chunk, chunk)
        pre = pre_self[rows, :] + dot(agg[rows, :], w_neigh[...])
        s = 0.5 * jnp.tanh(0.5 * pre) + 0.5
        value = pre * s
        out[rows, :] = value.astype(BF16)
        gpre[rows, :] = (cot[rows, :].astype(F32) * (s + value * (1.0 - s))).astype(BF16)

    term[:width, :] = dot(x_self_t[...], gpre[...]).astype(BF16)
    term[width:, :] = dot_tn(agg[...], gpre[...]).astype(BF16)

    def piece_of(ref, i, j):
        return ref.at[pl.ds(pl.multiple_of(i * grad_rows + j * piece, 16), piece), :]

    sent_g = [
        [
            send(
                piece_of(term, partner(me_g, k), j),
                part(term_in.at[j], k, piece),
                "group",
                me_g,
                k,
                send_g.at[j, k],
                recv_g.at[j, k],
            )
            for k in range(ngroup - 1, 0, -1)
        ]
        for j in range(parts)
    ]

    for i in range(masters // chunk):
        rows = pl.ds(i * chunk, chunk)
        g_agg = dot_nt(gpre[rows, :], w_neigh[...]).astype(BF16)
        g_rows[rows, :] = g_agg
        for k in range(chunk // edge):
            g_dest[i * chunk // edge + k] = g_agg[k * edge : (k + 1) * edge, :]
    back[...] = dot(pick_t[...], g_rows[...]).astype(BF16)
    sent_b = [
        send(
            part(back, k, capacity),
            part(mirror_grad, me_d, capacity),
            "dom",
            me_d,
            k,
            send_b.at[k],
            recv_b.at[k],
        )
        for k in [ndom // 2, *[k for i in range(1, ndom // 2) for k in (i, ndom // 2 + i)]]
    ]
    keep_b = pltpu.make_async_copy(
        part(back, 0, capacity), part(mirror_grad, me_d, capacity), local_sem.at[1]
    )
    keep_b.start()

    @pl.loop(0, masters // chunk)
    def _(i):
        rows = pl.ds(pl.multiple_of(i * chunk, chunk), chunk)
        dx_self[rows, :] = dot_nt(gpre[rows, :], w_self[...]).astype(BF16)

    for b in range(nblock):
        turned = tiles[b].T
        for c in range(nsrc // edge):
            backward[c * edge : (c + 1) * edge, b * edge : (b + 1) * edge] = kept(
                turned, col_of[b], c
            )

    def row_copy(j, i, to, owner):
        return pltpu.make_async_remote_copy(
            src_ref=rows_out.at[j],
            dst_ref=part(rows_in.at[j], owner, piece),
            send_sem=send_d.at[j, i],
            recv_sem=recv_d.at[j, owner],
            device_id={"dom": to},
            device_id_type=MESH,
        )

    sent_d = []
    for j in range(parts):
        for copy in sent_g[j]:
            copy.wait_recv()
        total = piece_of(term, me_g, j)[...].astype(F32)
        for k in range(1, ngroup):
            total = total + term_in[j, k * piece : (k + 1) * piece, :].astype(F32)
        rows_out[j] = total.astype(BF16)
        part(rows_in.at[j], me_d, piece)[...] = total.astype(BF16)
        for i in range(ndom - 1):
            to = i + (i >= me_d).astype(jnp.int32)
            row_copy(j, i, to, me_d).start()
            sent_d.append(row_copy(j, i, to, to))
    for copies in sent_g:
        for copy in copies:
            copy.wait_send()

    keep_b.wait()
    for copy in sent_b:
        copy.wait()
    for k in range(slots // edge):
        g_dest[master_tiles + k] = mirror_grad[k * edge : (k + 1) * edge, :]
    for b in range(nblock):
        chosen[b * edge : (b + 1) * edge, :] = g_dest[dest[b]]
    dx_src[...] = dot(backward[...], chosen[...]).astype(BF16)

    for copy in sent_d:
        copy.wait()
    for j in range(parts):
        total = rows_in[j, :piece, :].astype(F32)
        for k in range(1, ndom):
            total = total + rows_in[j, k * piece : (k + 1) * piece, :].astype(F32)
        grad_ref[j * piece : (j + 1) * piece, :] = total * factor


def results_kernel(*refs):
    sources, targets, sem = refs[:4], refs[4:8], refs[8]
    stores = [pltpu.make_async_copy(a, b, sem.at[i]) for i, (a, b) in enumerate(zip(sources, targets))]
    for store in stores:
        store.start()
    for store in stores:
        store.wait()


def on_device(
    x_self,
    x_src,
    tiles,
    slot_dest_row,
    block_col,
    block_count,
    mirror_count,
    mirror_index,
    cotangent,
    w_self,
    w_neigh,
):
    masters, width = x_self.shape
    nsrc = x_src.shape[0]
    nblock = tiles.shape[0]
    ndom = lax.axis_size("dom")
    ngroup = lax.axis_size("group")
    capacity = mirror_index.shape[2]
    slots = ndom * capacity
    dest = masters + slots
    span = nblock * TILE_EDGE
    grad_rows = 2 * width // ngroup
    parts = max(1, min(PARTS, grad_rows // 16))
    piece = grad_rows // parts
    vmem = pl.BlockSpec(memory_space=pltpu.VMEM)
    anywhere = pl.BlockSpec(memory_space=pl.ANY)
    hbm = pl.BlockSpec(memory_space=pltpu.HBM)
    factor = float((masters * ngroup * ndom) ** -0.5)

    def rows16(n, m=width):
        return pltpu.VMEM((n, m), BF16)

    def rows32(n, m=width):
        return pltpu.VMEM((n, m), F32)

    def dma(*shape):
        return pltpu.SemaphoreType.DMA(shape)

    arguments = [
        pltpu.with_memory_space_constraint(a, pltpu.HBM)
        for a in (
            slot_dest_row,
            block_col,
            mirror_count,
            mirror_index,
            tiles,
            x_src.reshape(nsrc // TILE_EDGE, TILE_EDGE, width),
            x_self,
            cotangent,
            w_self,
            w_neigh,
        )
    ]
    arguments.insert(2, block_count)
    in_specs = [hbm] * len(arguments)
    in_specs[2] = pl.BlockSpec(memory_space=pltpu.SMEM)
    result_shapes = (
        jax.ShapeDtypeStruct((masters, width), BF16),
        jax.ShapeDtypeStruct((masters, width), BF16),
        jax.ShapeDtypeStruct((nsrc, width), BF16),
        jax.ShapeDtypeStruct((grad_rows, width), F32),
    )
    results = pl.pallas_call(
        functools.partial(layer_kernel, ndom, ngroup, capacity, factor),
        out_shape=result_shapes,
        in_specs=in_specs,
        out_specs=(vmem,) * 4,
        scratch_shapes=[
            pltpu.SMEM((nblock,), jnp.int32),
            pltpu.SMEM((nblock,), jnp.int32),
            pltpu.SMEM((1, ndom), jnp.int32),
            pltpu.VMEM((1, ndom, capacity), jnp.int32),
            pltpu.VMEM((1, slots), jnp.int32),
            pltpu.VMEM(tiles.shape, BF16),
            pltpu.VMEM((nsrc // TILE_EDGE, TILE_EDGE, width), BF16),
            rows16(masters),
            rows16(masters),
            rows16(width),
            rows16(width),
            rows16(span),
            rows16(max(masters, slots), span),
            rows16(nsrc, span),
            rows16(masters, slots),
            rows16(slots, masters),
            rows16(slots),
            rows32(masters),
            rows32(masters),
            rows16(masters),
            rows16(masters),
            rows16(masters),
            pltpu.VMEM((dest // TILE_EDGE, TILE_EDGE, width), BF16),
            rows16(slots),
            rows16(slots),
            rows16(slots),
            rows16(width, masters),
            rows16(2 * width),
            pltpu.VMEM((parts, ngroup * piece, width), BF16),
            pltpu.VMEM((parts, piece, width), BF16),
            pltpu.VMEM((parts, ndom * piece, width), BF16),
            dma(10),
            dma(2),
            dma(ndom),
            dma(ndom),
            dma(ndom),
            dma(ndom),
            dma(parts, ngroup),
            dma(parts, ngroup),
            dma(parts, ndom),
            dma(parts, ndom),
        ],
        compiler_params=pltpu.CompilerParams(
            collective_id=0, has_side_effects=True, vmem_limit_bytes=VMEM_LIMIT
        ),
        name="layer",
    )(*arguments)
    return pl.pallas_call(
        results_kernel,
        out_shape=result_shapes,
        in_specs=[anywhere] * 4,
        out_specs=(hbm,) * 4,
        scratch_shapes=[dma(4)],
        compiler_params=pltpu.CompilerParams(vmem_limit_bytes=VMEM_LIMIT),
        name="results",
    )(*results)


def solution(mesh):
    return jax.shard_map(
        on_device,
        mesh=mesh,
        in_specs=(
            P(("group", "dom"), None),
            P(("group", "dom"), None),
            P(("group", "dom"), None, None),
            P(("group", "dom")),
            P(("group", "dom")),
            P(("group", "dom")),
            P(("group", "dom"), None),
            P(("group", "dom"), None, None),
            P(("group", "dom"), None),
            P(),
            P(),
        ),
        out_specs=(
            P(("group", "dom"), None),
            P(("group", "dom"), None),
            P(("group", "dom"), None),
            P("group", None),
        ),
        check_vma=False,
    )
```

```python
import functools

import jax
import jax.numpy as jnp
from jax import lax
from jax.experimental import pallas as pl
from jax.experimental.pallas import tpu as pltpu
from jax.sharding import PartitionSpec as P

TILE_EDGE = 128
VMEM_LIMIT = 48 * 2**20
PARTS = 1
MESH = pl.DeviceIdType.MESH
F32 = jnp.float32
BF16 = jnp.bfloat16


def dot(a, b):
    return jnp.dot(a, b, preferred_element_type=F32)


def dot_nt(a, b):
    return lax.dot_general(a, b, (((1,), (1,)), ((), ())), preferred_element_type=F32)


def dot_tn(a, b):
    return lax.dot_general(a, b, (((0,), (0,)), ((), ())), preferred_element_type=F32)


def partner(me, k):
    bit = 1
    while bit <= k:
        if k & bit:
            me = me + bit - 2 * bit * ((me // bit) % 2)
        bit *= 2
    return me


def layer_kernel(
    ndom,
    ngroup,
    capacity,
    factor,
    dest_hbm,
    col_hbm,
    count,
    live_hbm,
    index_hbm,
    tiles_hbm,
    x_src_hbm,
    x_self_hbm,
    cot_hbm,
    w_self_hbm,
    w_neigh_hbm,
    out,
    dx_self,
    dx_src,
    grad_ref,
    dest,
    col,
    live,
    index3,
    index,
    tiles,
    x_src,
    x_self,
    cot,
    w_self,
    w_neigh,
    chosen,
    forward,
    backward,
    pick,
    pick_t,
    mirror,
    own,
    pre_self,
    agg,
    gpre,
    g_rows,
    g_dest,
    mirror_grad,
    received,
    back,
    x_self_t,
    term,
    term_in,
    rows_out,
    rows_in,
    load_sem,
    local_sem,
    send_a,
    recv_a,
    send_b,
    recv_b,
    send_g,
    recv_g,
    send_d,
    recv_d,
):
    me_d = lax.axis_index("dom")
    me_g = lax.axis_index("group")
    masters, width = x_self.shape
    slots = index.shape[1]
    nblock = tiles.shape[0]
    nsrc = dx_src.shape[0]
    parts = term_in.shape[0]
    grad_rows = term.shape[0] // ngroup
    piece = grad_rows // parts
    half = slots // 2
    chunk = 256
    edge = TILE_EDGE
    master_tiles = masters // edge

    pairs = [
        (dest_hbm, dest),
        (col_hbm, col),
        (x_src_hbm, x_src),
        (tiles_hbm, tiles),
        (live_hbm, live),
        (index_hbm, index3),
        (x_self_hbm, x_self),
        (w_self_hbm, w_self),
        (w_neigh_hbm, w_neigh),
        (cot_hbm, cot),
    ]
    loads = [pltpu.make_async_copy(a, b, load_sem.at[i]) for i, (a, b) in enumerate(pairs)]
    for load in loads[:4]:
        load.start()

    barrier = pltpu.get_barrier_semaphore()
    for k in range(ndom - 1, 0, -1):
        pl.semaphore_signal(
            barrier, inc=1, device_id={"dom": partner(me_d, k)}, device_id_type=MESH
        )
    for k in range(ngroup - 1, 0, -1):
        pl.semaphore_signal(
            barrier, inc=1, device_id={"group": partner(me_g, k)}, device_id_type=MESH
        )
    for load in loads[4:]:
        load.start()

    def part(ref, i, rows):
        return ref.at[pl.ds(pl.multiple_of(i * rows, 16), rows), :]

    def send(src, dst, axis, me, k, sent, got):
        copy = pltpu.make_async_remote_copy(
            src_ref=src,
            dst_ref=dst,
            send_sem=sent,
            recv_sem=got,
            device_id={axis: partner(me, k)},
            device_id_type=MESH,
        )
        copy.start()
        return copy

    for load in loads[:4]:
        load.wait()
    row_of, col_of = [], []
    for b in range(nblock):
        alive = (b < count[0]).astype(jnp.int32)
        row_of.append(alive * (dest[b] + 1) - 1)
        col_of.append(alive * (col[b] + 1) - 1)
    for b in range(nblock):
        chosen[b * edge : (b + 1) * edge, :] = x_src[col[b]]

    def kept(tile, key, wanted):
        return tile * jnp.broadcast_to((key == wanted).astype(F32), tile.shape).astype(BF16)

    def spread(at, wanted):
        for b in range(nblock):
            forward[at * edge : (at + 1) * edge, b * edge : (b + 1) * edge] = kept(
                tiles[b], row_of[b], wanted
            )

    for m in range(slots // edge):
        spread(m, master_tiles + m)
    mirror[...] = dot(forward[:slots, :], chosen[...]).astype(BF16)

    pl.semaphore_wait(barrier, ndom + ngroup - 2)
    def mirror_copy(k, to):
        return pltpu.make_async_remote_copy(
            src_ref=part(mirror, to, capacity),
            dst_ref=part(received, k, capacity),
            send_sem=send_a.at[k],
            recv_sem=recv_a.at[k],
            device_id={"dom": to},
            device_id_type=MESH,
        )

    low = (me_d < ndom // 2).astype(jnp.int32)
    near = low * me_d + (1 - low) * (ndom - 1 - me_d)
    side = 1 - 2 * low
    for i in range(ndom - 1):
        both = (i < 2 * near).astype(jnp.int32)
        away = both * (i // 2 + 1) + (1 - both) * (i - near + 1)
        turn = both * (1 - 2 * (i % 2)) - (1 - both)
        to = me_d + turn * side * away
        k, bit = 0, 1
        while bit < ndom:
            k = k + bit * lax.rem(me_d // bit + to // bit, 2)
            bit *= 2
        mirror_copy(k, to).start()
    sent_a = [None] + [mirror_copy(k, partner(me_d, k)) for k in range(1, ndom)]
    keep_a = pltpu.make_async_copy(
        part(mirror, me_d, capacity), part(received, 0, capacity), local_sem.at[0]
    )
    keep_a.start()

    for load in loads[4:]:
        load.wait()
    lane = lax.broadcasted_iota(jnp.int32, (1, capacity), 1)
    for k in range(ndom):
        p = partner(me_d, k)
        index[:, k * capacity : (k + 1) * capacity] = jnp.where(
            lane < live[0, p], index3[0, pl.ds(p, 1), :], -1
        )
    index_row = index[...]

    for m in range(master_tiles):
        spread(m, m)

    @pl.loop(0, masters // chunk)
    def _(i):
        rows = pl.ds(pl.multiple_of(i * chunk, chunk), chunk)
        own[rows, :] = dot(forward[rows, :], chosen[...])
        pre_self[rows, :] = dot(x_self[rows, :], w_self[...])
        ids = lax.broadcasted_iota(jnp.int32, (chunk, slots), 0) + i * chunk
        pick[rows, :] = jnp.where(ids == index_row, 1.0, 0.0).astype(BF16)

    index_col = jnp.broadcast_to(index_row, (edge, slots)).T
    lanes = lax.broadcasted_iota(jnp.int32, (slots, edge), 1)
    for k in range(masters // edge):
        pick_t[:, k * edge : (k + 1) * edge] = jnp.where(
            lanes + k * edge == index_col, 1.0, 0.0
        ).astype(BF16)
    for k in range(masters // chunk):
        x_self_t[:, k * chunk : (k + 1) * chunk] = x_self[k * chunk : (k + 1) * chunk, :].T

    keep_a.wait()
    for k in range(1, ndom // 2):
        sent_a[k].wait()

    @pl.loop(0, masters // chunk)
    def _(i):
        rows = pl.ds(pl.multiple_of(i * chunk, chunk), chunk)
        own[rows, :] += dot(pick[rows, :half], received[:half, :])

    for k in range(ndom // 2, ndom):
        sent_a[k].wait()

    for i in range(masters // chunk):
        rows = pl.ds(i * chunk, chunk)
        agg[rows, :] = (own[rows, :] + dot(pick[rows, half:], received[half:, :])).astype(BF16)
    for i in range(masters // chunk):
        rows = pl.ds(i * chunk, chunk)
        pre = pre_self[rows, :] + dot(agg[rows, :], w_neigh[...])
        s = 0.5 * jnp.tanh(0.5 * pre) + 0.5
        value = pre * s
        out[rows, :] = value.astype(BF16)
        gpre[rows, :] = (cot[rows, :].astype(F32) * (s + value * (1.0 - s))).astype(BF16)

    term[:width, :] = dot(x_self_t[...], gpre[...]).astype(BF16)
    term[width:, :] = dot_tn(agg[...], gpre[...]).astype(BF16)

    def piece_of(ref, i, j):
        return ref.at[pl.ds(pl.multiple_of(i * grad_rows + j * piece, 16), piece), :]

    sent_g = [
        [
            send(
                piece_of(term, partner(me_g, k), j),
                part(term_in.at[j], k, piece),
                "group",
                me_g,
                k,
                send_g.at[j, k],
                recv_g.at[j, k],
            )
            for k in range(ngroup - 1, 0, -1)
        ]
        for j in range(parts)
    ]

    for i in range(masters // chunk):
        rows = pl.ds(i * chunk, chunk)
        g_agg = dot_nt(gpre[rows, :], w_neigh[...]).astype(BF16)
        g_rows[rows, :] = g_agg
        for k in range(chunk // edge):
            g_dest[i * chunk // edge + k] = g_agg[k * edge : (k + 1) * edge, :]
    back[...] = dot(pick_t[...], g_rows[...]).astype(BF16)
    sent_b = [
        send(
            part(back, k, capacity),
            part(mirror_grad, me_d, capacity),
            "dom",
            me_d,
            k,
            send_b.at[k],
            recv_b.at[k],
        )
        for k in [ndom // 2, *[k for i in range(1, ndom // 2) for k in (i, ndom // 2 + i)]]
    ]
    keep_b = pltpu.make_async_copy(
        part(back, 0, capacity), part(mirror_grad, me_d, capacity), local_sem.at[1]
    )
    keep_b.start()

    @pl.loop(0, masters // chunk)
    def _(i):
        rows = pl.ds(pl.multiple_of(i * chunk, chunk), chunk)
        dx_self[rows, :] = dot_nt(gpre[rows, :], w_self[...]).astype(BF16)

    for b in range(nblock):
        turned = tiles[b].T
        for c in range(nsrc // edge):
            backward[c * edge : (c + 1) * edge, b * edge : (b + 1) * edge] = kept(
                turned, col_of[b], c
            )

    def row_copy(j, i, to, owner):
        return pltpu.make_async_remote_copy(
            src_ref=rows_out.at[j],
            dst_ref=part(rows_in.at[j], owner, piece),
            send_sem=send_d.at[j, i],
            recv_sem=recv_d.at[j, owner],
            device_id={"dom": to},
            device_id_type=MESH,
        )

    sent_d = []
    for j in range(parts):
        for copy in sent_g[j]:
            copy.wait_recv()
        total = piece_of(term, me_g, j)[...].astype(F32)
        for k in range(1, ngroup):
            total = total + term_in[j, k * piece : (k + 1) * piece, :].astype(F32)
        rows_out[j] = total.astype(BF16)
        part(rows_in.at[j], me_d, piece)[...] = total.astype(BF16)
        for i in range(ndom - 1):
            to = i + (i >= me_d).astype(jnp.int32)
            row_copy(j, i, to, me_d).start()
            sent_d.append(row_copy(j, i, to, to))
    for copies in sent_g:
        for copy in copies:
            copy.wait_send()

    keep_b.wait()
    for copy in sent_b:
        copy.wait()
    for k in range(slots // edge):
        g_dest[master_tiles + k] = mirror_grad[k * edge : (k + 1) * edge, :]
    for b in range(nblock):
        chosen[b * edge : (b + 1) * edge, :] = g_dest[dest[b]]
    dx_src[...] = dot(backward[...], chosen[...]).astype(BF16)

    for copy in sent_d:
        copy.wait()
    for j in range(parts):
        total = rows_in[j, :piece, :].astype(F32)
        for k in range(1, ndom):
            total = total + rows_in[j, k * piece : (k + 1) * piece, :].astype(F32)
        grad_ref[j * piece : (j + 1) * piece, :] = total * factor


def results_kernel(*refs):
    sources, targets, sem = refs[:4], refs[4:8], refs[8]
    stores = [pltpu.make_async_copy(a, b, sem.at[i]) for i, (a, b) in enumerate(zip(sources, targets))]
    for store in stores:
        store.start()
    for store in stores:
        store.wait()


def on_device(
    x_self,
    x_src,
    tiles,
    slot_dest_row,
    block_col,
    block_count,
    mirror_count,
    mirror_index,
    cotangent,
    w_self,
    w_neigh,
):
    masters, width = x_self.shape
    nsrc = x_src.shape[0]
    nblock = tiles.shape[0]
    ndom = lax.axis_size("dom")
    ngroup = lax.axis_size("group")
    capacity = mirror_index.shape[2]
    slots = ndom * capacity
    dest = masters + slots
    span = nblock * TILE_EDGE
    grad_rows = 2 * width // ngroup
    parts = max(1, min(PARTS, grad_rows // 16))
    piece = grad_rows // parts
    vmem = pl.BlockSpec(memory_space=pltpu.VMEM)
    anywhere = pl.BlockSpec(memory_space=pl.ANY)
    hbm = pl.BlockSpec(memory_space=pltpu.HBM)
    factor = float((masters * ngroup * ndom) ** -0.5)

    def rows16(n, m=width):
        return pltpu.VMEM((n, m), BF16)

    def rows32(n, m=width):
        return pltpu.VMEM((n, m), F32)

    def dma(*shape):
        return pltpu.SemaphoreType.DMA(shape)

    arguments = [
        pltpu.with_memory_space_constraint(a, pltpu.HBM)
        for a in (
            slot_dest_row,
            block_col,
            mirror_count,
            mirror_index,
            tiles,
            x_src.reshape(nsrc // TILE_EDGE, TILE_EDGE, width),
            x_self,
            cotangent,
            w_self,
            w_neigh,
        )
    ]
    arguments.insert(2, block_count)
    in_specs = [hbm] * len(arguments)
    in_specs[2] = pl.BlockSpec(memory_space=pltpu.SMEM)
    result_shapes = (
        jax.ShapeDtypeStruct((masters, width), BF16),
        jax.ShapeDtypeStruct((masters, width), BF16),
        jax.ShapeDtypeStruct((nsrc, width), BF16),
        jax.ShapeDtypeStruct((grad_rows, width), F32),
    )
    results = pl.pallas_call(
        functools.partial(layer_kernel, ndom, ngroup, capacity, factor),
        out_shape=result_shapes,
        in_specs=in_specs,
        out_specs=(vmem,) * 4,
        scratch_shapes=[
            pltpu.SMEM((nblock,), jnp.int32),
            pltpu.SMEM((nblock,), jnp.int32),
            pltpu.SMEM((1, ndom), jnp.int32),
            pltpu.VMEM((1, ndom, capacity), jnp.int32),
            pltpu.VMEM((1, slots), jnp.int32),
            pltpu.VMEM(tiles.shape, BF16),
            pltpu.VMEM((nsrc // TILE_EDGE, TILE_EDGE, width), BF16),
            rows16(masters),
            rows16(masters),
            rows16(width),
            rows16(width),
            rows16(span),
            rows16(max(masters, slots), span),
            rows16(nsrc, span),
            rows16(masters, slots),
            rows16(slots, masters),
            rows16(slots),
            rows32(masters),
            rows32(masters),
            rows16(masters),
            rows16(masters),
            rows16(masters),
            pltpu.VMEM((dest // TILE_EDGE, TILE_EDGE, width), BF16),
            rows16(slots),
            rows16(slots),
            rows16(slots),
            rows16(width, masters),
            rows16(2 * width),
            pltpu.VMEM((parts, ngroup * piece, width), BF16),
            pltpu.VMEM((parts, piece, width), BF16),
            pltpu.VMEM((parts, ndom * piece, width), BF16),
            dma(10),
            dma(2),
            dma(ndom),
            dma(ndom),
            dma(ndom),
            dma(ndom),
            dma(parts, ngroup),
            dma(parts, ngroup),
            dma(parts, ndom),
            dma(parts, ndom),
        ],
        compiler_params=pltpu.CompilerParams(
            collective_id=0, has_side_effects=True, vmem_limit_bytes=VMEM_LIMIT
        ),
        name="layer",
    )(*arguments)
    return pl.pallas_call(
        results_kernel,
        out_shape=result_shapes,
        in_specs=[anywhere] * 4,
        out_specs=(hbm,) * 4,
        scratch_shapes=[dma(4)],
        compiler_params=pltpu.CompilerParams(vmem_limit_bytes=VMEM_LIMIT),
        name="results",
    )(*results)


def solution(mesh):
    return jax.shard_map(
        on_device,
        mesh=mesh,
        in_specs=(
            P(("group", "dom"), None),
            P(("group", "dom"), None),
            P(("group", "dom"), None, None),
            P(("group", "dom")),
            P(("group", "dom")),
            P(("group", "dom")),
            P(("group", "dom"), None),
            P(("group", "dom"), None, None),
            P(("group", "dom"), None),
            P(),
            P(),
        ),
        out_specs=(
            P(("group", "dom"), None),
            P(("group", "dom"), None),
            P(("group", "dom"), None),
            P("group", None),
        ),
        check_vma=False,
    )
```
